32 devices in a mesh: row: 4 (over y, x), col: 2 (over core), depth: 4 (over z).
Axes of the slice: x: 2, y: 2, z: 4, core: 2. Of those that a mesh axis runs over, the one named last changes fastest.
Arguments:
- features: bfloat16 [8192, 128], P(('row', 'col', 'depth')), may hold values from -6 to 6
- degree: int32 [8192], P(('row', 'col', 'depth')), may hold values from 4 to 32
- tiles: bfloat16 [4, 2, 4, 256, 128, 128], P('row', 'col', 'depth'), may hold values from 0 to 1, as said below
- tile_rows: int32 [4, 2, 4, 256], P('row', 'col', 'depth'), may hold values from 0 to 3
- tile_cols: int32 [4, 2, 4, 256], P('row', 'col', 'depth'), may hold values from 0 to 31
- tile_count: int32 [4, 2, 4], P('row', 'col', 'depth'), may hold values from 32 to 256, as said below
- weight: bfloat16 [128, 256], replicated, may hold values from -0.5 to 0.5
- bias: float32 [256], replicated, may hold values from -3 to 3
- cotangent: bfloat16 [8192, 256], P(('row', 'col', 'depth')), may hold values from -6 to 6
Outputs:
- hidden: bfloat16 [8192, 256], P(('row', 'col', 'depth'))
- weight_grad: float32 [128, 256], replicated
- bias_grad: float32 [256], replicated
- input_gradient: bfloat16 [8192, 128], P(('row', 'col', 'depth'))
The draws below stay inside these ranges and needn't reach their ends.
Inputs may be any that keep to these rules, and one draw needn't show every extreme that they name: `tile_count`: every device has 32 to 256 live slots, and some device has all 256. `tiles`: every entry is 0 or 1.
All inputs are finite; a program needn't handle non-finite values.
Results may differ from the reference program's by a relative error of at most 0.012.
Values may be sent and summed in bfloat16 or wider, within the bound.
A program may use at most 128 MiB of HBM per device.

```python
import jax
import jax.numpy as jnp
from jax import lax

FEATURES = 128
HIDDEN_SIZE = 256
TILE = 128
NODE_DEV = 256
TILE_DEV = 256
NODES = 8192
ROW_TILES = 4
COL_TILES = 32
N_ROW = 4
N_COL = 2
N_DEPTH = 4


def draw_tile_count(key, part):
    key = jax.random.fold_in(key, 7)
    first_key, second_key = jax.random.split(key)
    device_total = N_ROW * N_COL * N_DEPTH
    counts = jax.random.randint(first_key, (device_total,), TILE_DEV // 8, TILE_DEV + 1, dtype=jnp.int32)
    fullest = jax.random.randint(second_key, (), 0, device_total, dtype=jnp.int32)
    counts = counts.at[fullest].set(TILE_DEV)
    return counts.reshape(N_ROW, N_COL, N_DEPTH)


def draw_tiles(key, part):
    key = jax.random.fold_in(key, 11)
    density = 16.0 * ROW_TILES * N_ROW * N_DEPTH / (TILE * TILE_DEV * N_ROW * N_COL * N_DEPTH)
    density = min(density, 0.5)
    shape = (N_ROW, N_COL, N_DEPTH, TILE_DEV, TILE, TILE)
    marks = (jax.random.uniform(key, shape, jnp.float32) < density).astype(jnp.float32)
    return marks.astype(jnp.bfloat16)


def touch_ends(array, rng, low, high):
    longest = array.shape.index(max(array.shape))
    spots = []
    for shift in (0, 1):
        where = [jax.random.randint(jax.random.fold_in(rng, axis), (), 0, length) for axis, length in enumerate(array.shape)]
        where[longest] = (where[longest] + shift) % array.shape[longest]
        spots.append(tuple(where))
    return array.at[spots[0]].set(low).at[spots[1]].set(high)


def levels(key, shape, cuts, smallest, high):
    level = 1.0
    for axis_at, shards_of in cuts:
        heights = jax.random.uniform(jax.random.fold_in(jax.random.fold_in(key, 6), axis_at), (shards_of,), jnp.float32, smallest / len(cuts), high / len(cuts))
        level = level * jnp.repeat(jnp.exp(heights), shape[axis_at] // shards_of).reshape((-1,) + (1,) * (len(shape) - 1 - axis_at))
    return level


def scatter_about(rng, extent, scale, bound, cuts=(), held_as=jnp.bfloat16):
    values = jax.random.normal(rng, extent, jnp.float32) * scale
    if len(cuts) > 0:
        values = levels(rng, extent, cuts, -0.22, 0.18) * values
    return jnp.clip(values, min=-bound, max=bound).astype(held_as)


def setup_inputs(seed: int = 0) -> dict:
    key_list = jax.random.split(jax.random.key(seed), 10)
    features = scatter_about(key_list[0], (NODES, FEATURES), 1.0, 6.0, ((0, 32),))
    degree = touch_ends(jax.random.randint(key_list[1], (NODES,), 4, 33), jax.random.fold_in(key_list[1], 1), 4, 32).astype(jnp.int32)
    tiles = draw_tiles(jax.random.fold_in(key_list[9], 71), 0)
    tile_rows = touch_ends(jax.random.randint(key_list[3], (N_ROW, N_COL, N_DEPTH, TILE_DEV), 0, ROW_TILES), jax.random.fold_in(key_list[3], 1), 0, ROW_TILES - 1).astype(jnp.int32)
    tile_cols = touch_ends(jax.random.randint(key_list[4], (N_ROW, N_COL, N_DEPTH, TILE_DEV), 0, COL_TILES), jax.random.fold_in(key_list[4], 1), 0, COL_TILES - 1).astype(jnp.int32)
    tile_count = draw_tile_count(jax.random.fold_in(key_list[9], 71), 0)
    weight = scatter_about(key_list[6], (FEATURES, HIDDEN_SIZE), FEATURES ** -0.5, 0.5)
    bias = scatter_about(key_list[7], (HIDDEN_SIZE,), 0.5, 3.0, (), jnp.float32)
    cotangent = scatter_about(key_list[8], (NODES, HIDDEN_SIZE), 1.0, 6.0, ((0, 32),))
    return {"features": features, "degree": degree, "tiles": tiles, "tile_rows": tile_rows, "tile_cols": tile_cols, "tile_count": tile_count, "weight": weight, "bias": bias, "cotangent": cotangent}


def silu_parts(pre_act):
    sigma = jax.nn.sigmoid(pre_act)
    return (pre_act * sigma, sigma * (1.0 + pre_act * (1.0 - sigma)))

def reference(features, degree, tiles, tile_rows, tile_cols, tile_count, weight, bias, cotangent):
    device_total = N_ROW * N_COL * N_DEPTH
    largest_entry = lax.Precision.HIGHEST
    node_scale = lax.rsqrt(degree.astype(jnp.float32))[:, None]
    scaled = (features.astype(jnp.float32) * node_scale).astype(jnp.bfloat16)
    scaled_stretches = scaled.reshape(N_ROW, N_COL, N_DEPTH, NODE_DEV, FEATURES)
    flat_tiles = tiles.reshape(device_total, TILE_DEV, TILE, TILE)
    flat_rows = tile_rows.reshape(device_total, TILE_DEV)
    flat_cols = tile_cols.reshape(device_total, TILE_DEV)
    flat_count = tile_count.reshape(device_total)
    which_all = jnp.arange(device_total, dtype=jnp.int32)
    slot_ids = jnp.arange(TILE_DEV, dtype=jnp.int32)
    row_ids = jnp.arange(ROW_TILES, dtype=jnp.int32)
    col_ids = jnp.arange(COL_TILES, dtype=jnp.int32)

    def forward_step(carry, item):
        tile_block, rows_here, cols_here, live_count, which = item
        row_position = which // (N_COL * N_DEPTH)
        col_index = which // N_DEPTH % N_COL
        depth_index = which % N_DEPTH
        panel_rows = lax.dynamic_index_in_dim(scaled_stretches, col_index, 1, keepdims=False)
        panel_rows = panel_rows.reshape(COL_TILES, TILE, FEATURES)
        source = jnp.take(panel_rows, cols_here, axis=0)
        matmul_results = jnp.einsum('tab,tbf->taf', tile_block.astype(jnp.float32), source.astype(jnp.float32), precision=largest_entry)
        live_mask = (slot_ids < live_count).astype(jnp.float32)
        indicator_matrix = (rows_here[None, :] == row_ids[:, None]).astype(jnp.float32) * live_mask[None, :]
        partial_result = jnp.einsum('rt,taf->raf', indicator_matrix, matmul_results, precision=largest_entry)
        partial_result = partial_result.reshape(N_COL, NODE_DEV, FEATURES)
        return (carry.at[row_position, :, depth_index].add(partial_result), None)
    start_fwd = jnp.zeros((N_ROW, N_COL, N_DEPTH, NODE_DEV, FEATURES), jnp.float32)
    aggregate, _ = lax.scan(forward_step, start_fwd, (flat_tiles, flat_rows, flat_cols, flat_count, which_all))
    aggregate = aggregate.reshape(NODES, FEATURES)
    mixed = (node_scale * (aggregate + scaled.astype(jnp.float32))).astype(jnp.bfloat16)
    pre_act = jnp.dot(mixed, weight, preferred_element_type=jnp.float32) + bias.astype(jnp.float32)
    activated, slope_value = silu_parts(pre_act)
    hidden = activated.astype(jnp.bfloat16)
    pre_grad = (cotangent.astype(jnp.float32) * slope_value).astype(jnp.bfloat16)
    grad_norm = NODES ** (-0.5)
    weight_grad = lax.dot_general(mixed, pre_grad, (((0,), (0,)), ((), ())), preferred_element_type=jnp.float32) * grad_norm
    bias_grad = lax.optimization_barrier(jnp.sum(pre_grad.astype(jnp.float32), axis=0)) * grad_norm
    agg_grad = jnp.dot(pre_grad, weight.T, preferred_element_type=jnp.float32).astype(jnp.bfloat16)
    scaled_grad = (agg_grad.astype(jnp.float32) * node_scale).astype(jnp.bfloat16)
    grad_stretches = scaled_grad.reshape(N_ROW, N_COL, N_DEPTH, NODE_DEV, FEATURES)

    def backward_step(carry, item):
        tile_block, rows_here, cols_here, live_count, which = item
        row_position = which // (N_COL * N_DEPTH)
        col_index = which // N_DEPTH % N_COL
        depth_index = which % N_DEPTH
        group_rows = lax.dynamic_index_in_dim(grad_stretches, row_position, 0, keepdims=False)
        group_rows = lax.dynamic_index_in_dim(group_rows, depth_index, 1, keepdims=False)
        group_rows = group_rows.reshape(ROW_TILES, TILE, FEATURES)
        source = jnp.take(group_rows, rows_here, axis=0)
        matmul_results = jnp.einsum('tab,taf->tbf', tile_block.astype(jnp.float32), source.astype(jnp.float32), precision=largest_entry)
        live_mask = (slot_ids < live_count).astype(jnp.float32)
        indicator_matrix = (cols_here[None, :] == col_ids[:, None]).astype(jnp.float32) * live_mask[None, :]
        partial_result = jnp.einsum('qo,ovp->qvp', indicator_matrix, matmul_results, precision=largest_entry)
        partial_result = partial_result.reshape(N_ROW, N_DEPTH, NODE_DEV, FEATURES)
        return (carry.at[:, col_index].add(partial_result), None)
    back_sum, _ = lax.scan(backward_step, start_fwd, (flat_tiles, flat_rows, flat_cols, flat_count, which_all))
    back_sum = back_sum.reshape(NODES, FEATURES)
    input_gradient = (node_scale * (back_sum + scaled_grad.astype(jnp.float32))).astype(jnp.bfloat16)
    return (hidden, weight_grad, bias_grad, input_gradient)
```

```python
import functools

import jax
import jax.numpy as jnp
from jax import lax
from jax.experimental import pallas as pl
from jax.experimental.pallas import tpu as pltpu
from jax.sharding import PartitionSpec as P


def build_kernel(chunk, rows_ref, cols_ref, count_ref, tiles_ref, out_ref, held, sems):
    slots, tile, _ = held.shape
    live = count_ref[0]

    def fetch(k):
        part = pl.ds(k * chunk, chunk)
        return pltpu.make_async_copy(tiles_ref.at[part], held.at[part], sems.at[k])

    for k in range(slots // chunk):

        @pl.when(k * chunk < live)
        def _():
            fetch(k).start()

    zero = jnp.zeros((16, out_ref.shape[1]), out_ref.dtype)

    def clear(i, carry):
        out_ref[pl.ds(pl.multiple_of(i * 16, 16), 16), :] = zero
        return carry

    lax.fori_loop(0, out_ref.shape[0] // 16, clear, 0)

    def add(t, carry):
        at = (
            pl.ds(pl.multiple_of(rows_ref[t] * tile, tile), tile),
            pl.ds(pl.multiple_of(cols_ref[t] * tile, tile), tile),
        )
        out_ref[at] = out_ref[at] + held[t]
        return carry

    for k in range(slots // chunk):

        @pl.when(k * chunk < live)
        def _():
            fetch(k).wait()
            lax.fori_loop(k * chunk, jnp.minimum((k + 1) * chunk, live), add, 0)


def build_block(tiles, rows, cols, count, row_tiles, col_tiles):
    slots, tile, _ = tiles.shape
    chunk = 32
    shape = (row_tiles * tile, col_tiles * tile)
    smem = pl.BlockSpec(memory_space=pltpu.SMEM)
    return pl.pallas_call(
        functools.partial(build_kernel, chunk),
        out_shape=jax.ShapeDtypeStruct(shape, jnp.bfloat16),
        in_specs=[smem, smem, smem, pl.BlockSpec(memory_space=pl.ANY)],
        out_specs=pl.BlockSpec(memory_space=pltpu.VMEM),
        scratch_shapes=[
            pltpu.VMEM(tiles.shape, tiles.dtype),
            pltpu.SemaphoreType.DMA((slots // chunk,)),
        ],
        compiler_params=pltpu.CompilerParams(vmem_limit_bytes=56 * 1024 * 1024),
        cost_estimate=pl.CostEstimate(
            flops=tiles.size, bytes_accessed=tiles.size * 2 + shape[0] * shape[1] * 2, transcendentals=0
        ),
    )(rows, cols, count, tiles)


def silu_parts(pre_act):
    sigma = jax.nn.sigmoid(pre_act)
    return (pre_act * sigma, sigma * (1.0 + pre_act * (1.0 - sigma)))


def dense_part(mixed, weight, bias, cotangent):
    pre_act = jnp.dot(mixed, weight, preferred_element_type=jnp.float32) + bias
    activated, slope_value = silu_parts(pre_act)
    hidden = activated.astype(jnp.bfloat16)
    pre_grad = (cotangent.astype(jnp.float32) * slope_value).astype(jnp.bfloat16)
    weight_part = lax.dot_general(
        mixed, pre_grad, (((0,), (0,)), ((), ())), preferred_element_type=jnp.float32
    )
    bias_portion = jnp.sum(pre_grad.astype(jnp.float32), axis=0)
    agg_grad = jnp.dot(pre_grad, weight.T, preferred_element_type=jnp.float32).astype(jnp.bfloat16)
    return (hidden, weight_part, bias_portion, agg_grad)


def local(features, degree, tiles, tile_rows, tile_cols, tile_count, weight, bias, cotangent):
    node_dev, feature_width = features.shape
    tile_size = tiles.shape[-1]
    slot_total = tiles.shape[3]
    col_total = lax.axis_size("col")
    row_tiles = col_total * node_dev // tile_size
    span = lax.axis_size(("row", "depth")) * node_dev // tile_size
    node_total = node_dev * lax.axis_size(("row", "col", "depth"))
    grad_norm = node_total ** (-0.5)
    node_scale = lax.rsqrt(degree.astype(jnp.float32))[:, None]
    scaled = (features.astype(jnp.float32) * node_scale).astype(jnp.bfloat16)
    panel_rows = lax.all_gather(scaled, ("row", "depth"), axis=0, tiled=True)
    block = build_block(
        tiles.reshape(slot_total, tile_size, tile_size),
        tile_rows.reshape(slot_total),
        tile_cols.reshape(slot_total),
        tile_count.reshape(1),
        row_tiles,
        span,
    )
    partial_result = jnp.dot(block, panel_rows, preferred_element_type=jnp.float32)
    aggregate = lax.psum_scatter(partial_result, "col", scatter_dimension=0, tiled=True)
    mixed = (node_scale * (aggregate + scaled.astype(jnp.float32))).astype(jnp.bfloat16)
    hidden, weight_part, bias_portion, agg_grad = dense_part(mixed, weight, bias, cotangent)
    weight_grad, bias_grad = lax.psum((weight_part, bias_portion), ("row", "col", "depth"))
    scaled_grad = (agg_grad.astype(jnp.float32) * node_scale).astype(jnp.bfloat16)
    group_grad = lax.all_gather(scaled_grad, "col", axis=0, tiled=True)
    terms = lax.dot_general(
        block, group_grad, (((0,), (0,)), ((), ())), preferred_element_type=jnp.float32
    )
    back_sum = lax.psum_scatter(terms, ("row", "depth"), scatter_dimension=0, tiled=True)
    input_gradient = (node_scale * (back_sum + scaled_grad.astype(jnp.float32))).astype(
        jnp.bfloat16
    )
    return (hidden, weight_grad * grad_norm, bias_grad * grad_norm, input_gradient)


def solution(mesh):
    return jax.shard_map(
        local,
        mesh=mesh,
        in_specs=(
            P(("row", "col", "depth"), None),
            P(("row", "col", "depth")),
            P("row", "col", "depth", None, None, None),
            P("row", "col", "depth", None),
            P("row", "col", "depth", None),
            P("row", "col", "depth"),
            P(),
            P(),
            P(("row", "col", "depth"), None),
        ),
        out_specs=(P(("row", "col", "depth"), None), P(), P(), P(("row", "col", "depth"), None)),
        check_vma=False,
    )
```

```python
import functools

import jax
import jax.numpy as jnp
from jax import lax
from jax.experimental import pallas as pl
from jax.experimental.pallas import tpu as pltpu
from jax.sharding import PartitionSpec as P


def build_kernel(chunk, rows_ref, cols_ref, count_ref, tiles_ref, out_ref, held, sems):
    slots, tile, _ = held.shape
    live = count_ref[0]

    def fetch(k):
        part = pl.ds(k * chunk, chunk)
        return pltpu.make_async_copy(tiles_ref.at[part], held.at[part], sems.at[k])

    for k in range(slots // chunk):

        @pl.when(k * chunk < live)
        def _():
            fetch(k).start()

    zero = jnp.zeros((16, out_ref.shape[1]), out_ref.dtype)

    def clear(i, carry):
        out_ref[pl.ds(pl.multiple_of(i * 16, 16), 16), :] = zero
        return carry

    lax.fori_loop(0, out_ref.shape[0] // 16, clear, 0)

    def add(t, carry):
        at = (
            pl.ds(pl.multiple_of(rows_ref[t] * tile, tile), tile),
            pl.ds(pl.multiple_of(cols_ref[t] * tile, tile), tile),
        )
        out_ref[at] = out_ref[at] + held[t]
        return carry

    for k in range(slots // chunk):

        @pl.when(k * chunk < live)
        def _():
            fetch(k).wait()
            lax.fori_loop(k * chunk, jnp.minimum((k + 1) * chunk, live), add, 0)


def build_block(tiles, rows, cols, count, row_tiles, col_tiles):
    slots, tile, _ = tiles.shape
    chunk = 32
    shape = (row_tiles * tile, col_tiles * tile)
    smem = pl.BlockSpec(memory_space=pltpu.SMEM)
    return pl.pallas_call(
        functools.partial(build_kernel, chunk),
        out_shape=jax.ShapeDtypeStruct(shape, jnp.bfloat16),
        in_specs=[smem, smem, smem, pl.BlockSpec(memory_space=pl.ANY)],
        out_specs=pl.BlockSpec(memory_space=pltpu.VMEM),
        scratch_shapes=[
            pltpu.VMEM(tiles.shape, tiles.dtype),
            pltpu.SemaphoreType.DMA((slots // chunk,)),
        ],
        compiler_params=pltpu.CompilerParams(vmem_limit_bytes=56 * 1024 * 1024),
        cost_estimate=pl.CostEstimate(
            flops=tiles.size, bytes_accessed=tiles.size * 2 + shape[0] * shape[1] * 2, transcendentals=0
        ),
    )(rows, cols, count, tiles)


def silu_parts(pre_act):
    sigma = jax.nn.sigmoid(pre_act)
    return (pre_act * sigma, sigma * (1.0 + pre_act * (1.0 - sigma)))


def layer_kernel(
    sizes,
    grad_norm,
    block,
    features,
    scale,
    weight,
    bias,
    cotangent,
    hidden,
    weight_grad,
    bias_grad,
    input_gradient,
    panel,
    acc,
    share,
    grads,
    back_own,
    back_send,
    back_row,
    deep_send,
    deep_recv,
    w_send,
    w_col,
    w_row,
    w_deep,
    w_out,
    panel_s,
    panel_r,
    share_s,
    share_r,
    grads_s,
    grads_r,
    back_s,
    back_r,
    deep_s,
    deep_r,
    wc_s,
    wc_r,
    wr_s,
    wr_r,
    wd_s,
    wd_r,
    wo_s,
    wo_r,
):
    rows, cols, depths = sizes
    nodes = features.shape[0]
    me_r, me_c, me_d = (lax.axis_index(name) for name in ("row", "col", "depth"))
    f32, bf16 = jnp.float32, jnp.bfloat16

    def row_of(j):
        return lax.rem(me_r + j, rows)

    def col_of(m):
        return lax.rem(me_c + m, cols)

    def deep_of(k):
        return lax.rem(me_d + k, depths)

    def send(src, dst, send_sem, recv_sem, **peer):
        return pltpu.make_async_remote_copy(
            src_ref=src,
            dst_ref=dst,
            send_sem=send_sem,
            recv_sem=recv_sem,
            device_id=peer,
            device_id_type=pl.DeviceIdType.MESH,
        )

    sent = []

    def start(*args, **peer):
        copy = send(*args, **peer)
        copy.start()
        sent.append(copy)

    deep_order = sorted(range(1, depths), key=lambda k: (min(k, depths - k), k))

    barrier = pltpu.get_barrier_semaphore()
    for m in range(1, cols):
        pl.semaphore_signal(barrier, inc=1, device_id={"col": col_of(m)}, device_id_type=pl.DeviceIdType.MESH)
    for j in range(1, rows):
        pl.semaphore_signal(barrier, inc=1, device_id={"row": row_of(j)}, device_id_type=pl.DeviceIdType.MESH)
    for k in range(1, depths):
        pl.semaphore_signal(barrier, inc=1, device_id={"depth": deep_of(k)}, device_id_type=pl.DeviceIdType.MESH)
    mine = me_r * depths + me_d
    scaled = (features[...].astype(f32) * scale[...]).astype(bf16)
    panel[mine] = scaled
    pl.semaphore_wait(barrier, cols + rows + depths - 3)

    for k in deep_order:
        start(panel.at[mine], panel.at[mine], panel_s.at[k, 0], panel_r.at[mine], depth=deep_of(k))
    for j in range(1, rows):
        start(panel.at[mine], panel.at[mine], panel_s.at[0, j], panel_r.at[mine], row=row_of(j))

    def product(q):
        at = pl.ds(pl.multiple_of(q * nodes, nodes), nodes)
        return jnp.dot(block[:, at], panel[q], preferred_element_type=f32)

    acc[...] = product(mine)
    for k in deep_order:
        q = me_r * depths + deep_of(k)
        send(panel.at[q], panel.at[q], panel_s.at[k, 0], panel_r.at[q], depth=deep_of(k)).wait_recv()
        for j in range(1, rows):
            start(panel.at[q], panel.at[q], panel_s.at[k, j], panel_r.at[q], row=row_of(j))
        acc[...] += product(q)
    for k in [0] + deep_order:
        for j in range(1, rows):
            q = row_of(j) * depths + deep_of(k)
            send(panel.at[q], panel.at[q], panel_s.at[k, j], panel_r.at[q], row=row_of(j)).wait_recv()
            acc[...] += product(q)

    def acc_of(c):
        return acc.at[pl.ds(pl.multiple_of(c * nodes, nodes), nodes)]

    for m in range(1, cols):
        start(acc_of(col_of(m)), share.at[m - 1], share_s.at[m - 1], share_r.at[m - 1], col=col_of(m))
    aggregate = acc_of(me_c)[...]
    for m in range(1, cols):
        send(acc_of(me_c), share.at[m - 1], share_s.at[m - 1], share_r.at[m - 1], col=col_of(m)).wait_recv()
        aggregate = aggregate + share[m - 1]

    mixed = (scale[...] * (aggregate + scaled.astype(f32))).astype(bf16)
    pre_act = jnp.dot(mixed, weight[...], preferred_element_type=f32) + bias[...]
    activated, slope_value = silu_parts(pre_act)
    hidden[...] = activated.astype(bf16)
    pre_grad = (cotangent[...].astype(f32) * slope_value).astype(bf16)
    agg_grad = lax.dot_general(
        pre_grad, weight[...], (((1,), (1,)), ((), ())), preferred_element_type=f32
    ).astype(bf16)
    scaled_grad = (agg_grad.astype(f32) * scale[...]).astype(bf16)
    grads[me_c] = scaled_grad
    for m in range(1, cols):
        start(grads.at[me_c], grads.at[me_c], grads_s.at[m - 1], grads_r.at[m - 1], col=col_of(m))

    w_part = lax.dot_general(mixed, pre_grad, (((0,), (0,)), ((), ())), preferred_element_type=f32)
    b_part = jnp.sum(pre_grad.astype(f32).reshape(nodes // 8, 8, pre_grad.shape[1]), axis=0)
    band = w_part.shape[0] // cols
    for c in range(cols):
        w_send[c, :band] = w_part[c * band : (c + 1) * band]
        w_send[c, band:] = b_part
    for m in range(1, cols):
        start(w_send.at[col_of(m)], w_col.at[me_c], wc_s.at[m - 1], wc_r.at[m - 1], col=col_of(m))
    w_col[me_c] = w_send[me_c]

    for m in range(1, cols):
        c = lax.rem(me_c + cols - m, cols)
        send(grads.at[c], grads.at[c], grads_s.at[m - 1], grads_r.at[m - 1], col=col_of(m)).wait_recv()
    turned = grads[...].reshape(cols * nodes, scaled_grad.shape[1]).T

    for k in deep_order + [0]:
        for j in list(range(1, rows)) + [0]:
            q = row_of(j) * depths + deep_of(k)
            at = pl.ds(pl.multiple_of(q * nodes, nodes), nodes)
            term = jnp.dot(turned, block[:, at], preferred_element_type=f32)
            if j == 0:
                back_own[k] = term
            else:
                back_send[k, j - 1] = term.astype(bf16)
                start(
                    back_send.at[k, j - 1],
                    back_row.at[k, j - 1],
                    back_s.at[k, j - 1],
                    back_r.at[k, j - 1],
                    row=row_of(j),
                )

    def total(buffer, count):
        value = buffer[0]
        for i in range(1, count):
            value = value + buffer[i]
        return value

    for m in range(1, cols):
        send(w_send.at[me_c], w_col.at[me_c], wc_s.at[m - 1], wc_r.at[m - 1], col=col_of(m)).wait_recv()
    w_row[me_r] = total(w_col, cols)
    for j in range(1, rows):
        start(w_row.at[me_r], w_row.at[me_r], wr_s.at[j - 1], wr_r.at[j - 1], row=row_of(j))

    def row_sum(k):
        value = back_own[k]
        for j in range(1, rows):
            send(
                back_send.at[k, j - 1],
                back_row.at[k, j - 1],
                back_s.at[k, j - 1],
                back_r.at[k, j - 1],
                row=row_of(j),
            ).wait_recv()
            value = value + back_row[k, j - 1].astype(f32)
        return value

    for k in deep_order:
        deep_send[k - 1] = row_sum(k).astype(bf16)
        start(deep_send.at[k - 1], deep_recv.at[k - 1], deep_s.at[k - 1], deep_r.at[k - 1], depth=deep_of(k))

    for j in range(1, rows):
        send(w_row.at[me_r], w_row.at[row_of(rows - j)], wr_s.at[j - 1], wr_r.at[j - 1], row=row_of(j)).wait_recv()
    w_deep[me_d] = total(w_row, rows)
    for k in range(1, depths):
        start(w_deep.at[me_d], w_deep.at[me_d], wd_s.at[k - 1], wd_r.at[k - 1], depth=deep_of(k))

    back = row_sum(0)

    for k in range(1, depths):
        send(
            w_deep.at[me_d], w_deep.at[deep_of(depths - k)], wd_s.at[k - 1], wd_r.at[k - 1], depth=deep_of(k)
        ).wait_recv()
    w_total = total(w_deep, depths) * grad_norm
    w_out[me_c] = w_total[:band]
    bias_grad[...] = jnp.sum(w_total[band:], axis=0, keepdims=True)
    for m in range(1, cols):
        start(w_out.at[me_c], w_out.at[me_c], wo_s.at[m - 1], wo_r.at[m - 1], col=col_of(m))

    for k in range(1, depths):
        send(
            deep_send.at[k - 1], deep_recv.at[k - 1], deep_s.at[k - 1], deep_r.at[k - 1], depth=deep_of(k)
        ).wait_recv()
        back = back + deep_recv[k - 1].astype(f32)
    input_gradient[...] = (scale[...] * (back.T + grads[me_c].astype(f32))).astype(bf16)

    for m in range(1, cols):
        c = lax.rem(me_c + cols - m, cols)
        send(w_out.at[c], w_out.at[c], wo_s.at[m - 1], wo_r.at[m - 1], col=col_of(m)).wait_recv()
    for c in range(cols):
        weight_grad[c * band : (c + 1) * band] = w_out[c]
    for copy in sent:
        copy.wait_send()


def run_layer(sizes, grad_norm, block, features, scale, weight, bias, cotangent):
    rows, cols, depths = sizes
    nodes, width = features.shape
    wide = weight.shape[1]
    band = width // cols
    f32, bf16 = jnp.float32, jnp.bfloat16

    def dma(*shape):
        return [pltpu.SemaphoreType.DMA(shape)] * 2

    return pl.pallas_call(
        functools.partial(layer_kernel, sizes, grad_norm),
        out_shape=(
            jax.ShapeDtypeStruct((nodes, wide), bf16),
            jax.ShapeDtypeStruct((width, wide), f32),
            jax.ShapeDtypeStruct((1, wide), f32),
            jax.ShapeDtypeStruct((nodes, width), bf16),
        ),
        in_specs=[pl.BlockSpec(memory_space=pltpu.VMEM)] * 6,
        out_specs=(pl.BlockSpec(memory_space=pltpu.VMEM),) * 4,
        scratch_shapes=[
            pltpu.VMEM((rows * depths, nodes, width), bf16),
            pltpu.VMEM((cols * nodes, width), f32),
            pltpu.VMEM((cols - 1, nodes, width), f32),
            pltpu.VMEM((cols, nodes, width), bf16),
            pltpu.VMEM((depths, width, nodes), f32),
            pltpu.VMEM((depths, rows - 1, width, nodes), bf16),
            pltpu.VMEM((depths, rows - 1, width, nodes), bf16),
            pltpu.VMEM((depths - 1, width, nodes), bf16),
            pltpu.VMEM((depths - 1, width, nodes), bf16),
            pltpu.VMEM((cols, band + 8, wide), f32),
            pltpu.VMEM((cols, band + 8, wide), f32),
            pltpu.VMEM((rows, band + 8, wide), f32),
            pltpu.VMEM((depths, band + 8, wide), f32),
            pltpu.VMEM((cols, band, wide), f32),
            pltpu.SemaphoreType.DMA((depths, rows)),
            pltpu.SemaphoreType.DMA((rows * depths,)),
            *dma(cols - 1),
            *dma(cols - 1),
            *dma(depths, rows - 1),
            *dma(depths - 1),
            *dma(cols - 1),
            *dma(rows - 1),
            *dma(depths - 1),
            *dma(cols - 1),
        ],
        compiler_params=pltpu.CompilerParams(
            collective_id=0, has_side_effects=True, vmem_limit_bytes=56 * 1024 * 1024
        ),
    )(block, features, scale, weight, bias, cotangent)


def local(features, degree, tiles, tile_rows, tile_cols, tile_count, weight, bias, cotangent):
    node_dev, feature_width = features.shape
    tile_size = tiles.shape[-1]
    slot_total = tiles.shape[3]
    sizes = tuple(lax.axis_size(name) for name in ("row", "col", "depth"))
    row_tiles = sizes[1] * node_dev // tile_size
    span = sizes[0] * sizes[2] * node_dev // tile_size
    grad_norm = (node_dev * sizes[0] * sizes[1] * sizes[2]) ** (-0.5)
    scale = jnp.broadcast_to(lax.rsqrt(degree.astype(jnp.float32))[:, None], features.shape)
    block = build_block(
        tiles.reshape(slot_total, tile_size, tile_size),
        tile_rows.reshape(slot_total),
        tile_cols.reshape(slot_total),
        tile_count.reshape(1),
        row_tiles,
        span,
    )
    hidden, weight_grad, bias_grad, input_gradient = run_layer(
        sizes, grad_norm, block, features, scale, weight, bias.reshape(1, -1), cotangent
    )
    return (hidden, weight_grad, bias_grad.reshape(-1), input_gradient)


def solution(mesh):
    return jax.shard_map(
        local,
        mesh=mesh,
        in_specs=(
            P(("row", "col", "depth"), None),
            P(("row", "col", "depth")),
            P("row", "col", "depth", None, None, None),
            P("row", "col", "depth", None),
            P("row", "col", "depth", None),
            P("row", "col", "depth"),
            P(),
            P(),
            P(("row", "col", "depth"), None),
        ),
        out_specs=(P(("row", "col", "depth"), None), P(), P(), P(("row", "col", "depth"), None)),
        check_vma=False,
    )
```

```python
import functools

import jax
import jax.numpy as jnp
from jax import lax
from jax.experimental import pallas as pl
from jax.experimental.pallas import tpu as pltpu
from jax.sharding import PartitionSpec as P


def build_kernel(chunk, rows_ref, cols_ref, count_ref, tiles_ref, out_ref, held, sems):
    slots, tile, _ = held.shape
    live = count_ref[0]

    def fetch(k):
        part = pl.ds(k * chunk, chunk)
        return pltpu.make_async_copy(tiles_ref.at[part], held.at[part], sems.at[k])

    for k in range(slots // chunk):

        @pl.when(k * chunk < live)
        def _():
            fetch(k).start()

    zero = jnp.zeros((16, out_ref.shape[1]), out_ref.dtype)

    def clear(i, carry):
        out_ref[pl.ds(pl.multiple_of(i * 16, 16), 16), :] = zero
        return carry

    lax.fori_loop(0, out_ref.shape[0] // 16, clear, 0)

    def add(t, carry):
        at = (
            pl.ds(pl.multiple_of(rows_ref[t] * tile, tile), tile),
            pl.ds(pl.multiple_of(cols_ref[t] * tile, tile), tile),
        )
        out_ref[at] = out_ref[at] + held[t]
        return carry

    for k in range(slots // chunk):

        @pl.when(k * chunk < live)
        def _():
            fetch(k).wait()
            lax.fori_loop(k * chunk, jnp.minimum((k + 1) * chunk, live), add, 0)


def build_block(tiles, rows, cols, count, row_tiles, col_tiles):
    slots, tile, _ = tiles.shape
    chunk = 32
    shape = (row_tiles * tile, col_tiles * tile)
    smem = pl.BlockSpec(memory_space=pltpu.SMEM)
    return pl.pallas_call(
        functools.partial(build_kernel, chunk),
        out_shape=jax.ShapeDtypeStruct(shape, jnp.bfloat16),
        in_specs=[smem, smem, smem, pl.BlockSpec(memory_space=pl.ANY)],
        out_specs=pl.BlockSpec(memory_space=pltpu.VMEM),
        scratch_shapes=[
            pltpu.VMEM(tiles.shape, tiles.dtype),
            pltpu.SemaphoreType.DMA((slots // chunk,)),
        ],
        compiler_params=pltpu.CompilerParams(vmem_limit_bytes=56 * 1024 * 1024),
        cost_estimate=pl.CostEstimate(
            flops=tiles.size, bytes_accessed=tiles.size * 2 + shape[0] * shape[1] * 2, transcendentals=0
        ),
    )(rows, cols, count, tiles)


def silu_parts(pre_act):
    sigma = jax.nn.sigmoid(pre_act)
    return (pre_act * sigma, sigma * (1.0 + pre_act * (1.0 - sigma)))


def layer_kernel(
    sizes,
    grad_norm,
    block_hbm,
    features,
    degree,
    weight,
    bias,
    cotangent,
    hidden,
    weight_grad,
    bias_grad,
    input_gradient,
    block,
    scale,
    panel,
    acc,
    share,
    grads,
    back_own,
    back_send,
    back_row,
    deep_send,
    deep_recv,
    w_send,
    w_col,
    w_mid,
    w_row,
    w_deep,
    w_out,
    block_s,
    panel_s,
    panel_r,
    share_s,
    share_r,
    grads_s,
    grads_r,
    back_s,
    back_r,
    deep_s,
    deep_r,
    wc_s,
    wc_r,
    wr_s,
    wr_r,
    wd_s,
    wd_r,
    wg_s,
    wg_r,
    wo_s,
    wo_r,
):
    rows, cols, depths = sizes
    nodes = features.shape[0]
    me_r, me_c, me_d = (lax.axis_index(name) for name in ("row", "col", "depth"))
    f32, bf16 = jnp.float32, jnp.bfloat16

    def row_of(j):
        return lax.rem(me_r + j, rows)

    def col_of(m):
        return lax.rem(me_c + m, cols)

    def deep_of(k):
        return lax.rem(me_d + k, depths)

    def send(src, dst, send_sem, recv_sem, **peer):
        return pltpu.make_async_remote_copy(
            src_ref=src,
            dst_ref=dst,
            send_sem=send_sem,
            recv_sem=recv_sem,
            device_id=peer,
            device_id_type=pl.DeviceIdType.MESH,
        )

    sent = []

    def start(*args, **peer):
        copy = send(*args, **peer)
        copy.start()
        sent.append(copy)

    deep_order = sorted(range(1, depths), key=lambda k: (min(k, depths - k), k))

    bring = pltpu.make_async_copy(block_hbm, block, block_s)
    bring.start()
    barrier = pltpu.get_barrier_semaphore()
    for m in range(1, cols):
        pl.semaphore_signal(barrier, inc=1, device_id={"col": col_of(m)}, device_id_type=pl.DeviceIdType.MESH)
    for j in range(1, rows):
        pl.semaphore_signal(barrier, inc=1, device_id={"row": row_of(j)}, device_id_type=pl.DeviceIdType.MESH)
    for k in range(1, depths):
        pl.semaphore_signal(barrier, inc=1, device_id={"depth": deep_of(k)}, device_id_type=pl.DeviceIdType.MESH)
    mine = me_r * depths + me_d
    node_scale = lax.rsqrt(degree[...].astype(f32))
    scale[...] = jnp.broadcast_to(node_scale, features.shape[::-1]).T
    scaled = (features[...].astype(f32) * scale[...]).astype(bf16)
    panel[mine] = scaled
    pl.semaphore_wait(barrier, cols + rows + depths - 3)

    for k in deep_order:
        start(panel.at[mine], panel.at[mine], panel_s.at[k, 0], panel_r.at[mine], depth=deep_of(k))
    for j in range(1, rows):
        start(panel.at[mine], panel.at[mine], panel_s.at[0, j], panel_r.at[mine], row=row_of(j))

    def product(q):
        at = pl.ds(pl.multiple_of(q * nodes, nodes), nodes)
        return jnp.dot(block[:, at], panel[q], preferred_element_type=f32)

    bring.wait()
    acc[...] = product(mine)
    for k in deep_order:
        q = me_r * depths + deep_of(k)
        send(panel.at[q], panel.at[q], panel_s.at[k, 0], panel_r.at[q], depth=deep_of(k)).wait_recv()
        for j in range(1, rows):
            start(panel.at[q], panel.at[q], panel_s.at[k, j], panel_r.at[q], row=row_of(j))
        acc[...] += product(q)
    for k in [0] + deep_order:
        for j in range(1, rows):
            q = row_of(j) * depths + deep_of(k)
            send(panel.at[q], panel.at[q], panel_s.at[k, j], panel_r.at[q], row=row_of(j)).wait_recv()
            acc[...] += product(q)

    def acc_of(c):
        return acc.at[pl.ds(pl.multiple_of(c * nodes, nodes), nodes)]

    for m in range(1, cols):
        start(acc_of(col_of(m)), share.at[m - 1], share_s.at[m - 1], share_r.at[m - 1], col=col_of(m))
    aggregate = acc_of(me_c)[...]
    for m in range(1, cols):
        send(acc_of(me_c), share.at[m - 1], share_s.at[m - 1], share_r.at[m - 1], col=col_of(m)).wait_recv()
        aggregate = aggregate + share[m - 1]

    mixed = (scale[...] * (aggregate + scaled.astype(f32))).astype(bf16)
    pre_act = jnp.dot(mixed, weight[...], preferred_element_type=f32) + bias[...]
    activated, slope_value = silu_parts(pre_act)
    hidden[...] = activated.astype(bf16)
    pre_grad = (cotangent[...].astype(f32) * slope_value).astype(bf16)
    agg_grad = lax.dot_general(
        pre_grad, weight[...], (((1,), (1,)), ((), ())), preferred_element_type=f32
    ).astype(bf16)
    scaled_grad = (agg_grad.astype(f32) * scale[...]).astype(bf16)
    grads[me_c] = scaled_grad
    for m in range(1, cols):
        start(grads.at[me_c], grads.at[me_c], grads_s.at[m - 1], grads_r.at[m - 1], col=col_of(m))

    w_part = lax.dot_general(mixed, pre_grad, (((0,), (0,)), ((), ())), preferred_element_type=f32)
    b_part = jnp.sum(pre_grad.astype(f32).reshape(nodes // 8, 8, pre_grad.shape[1]), axis=0)
    band = w_part.shape[0] // (cols * rows)
    for c in range(cols):
        for r in range(rows):
            first = (c * rows + r) * band
            w_send[c, r, :8] = b_part
            w_send[c, r, 8:] = w_part[first : first + band]
    for m in range(1, cols):
        start(w_send.at[col_of(m)], w_col.at[me_c], wc_s.at[m - 1], wc_r.at[m - 1], col=col_of(m))
    w_col[me_c] = w_send[me_c]

    for m in range(1, cols):
        c = lax.rem(me_c + cols - m, cols)
        send(grads.at[c], grads.at[c], grads_s.at[m - 1], grads_r.at[m - 1], col=col_of(m)).wait_recv()
    turned = grads[...].reshape(cols * nodes, scaled_grad.shape[1]).T

    def total(buffer, count):
        value = buffer[0]
        for i in range(1, count):
            value = value + buffer[i]
        return value

    for m in range(1, cols):
        c = lax.rem(me_c + cols - m, cols)
        send(w_send.at[c], w_col.at[c], wc_s.at[m - 1], wc_r.at[m - 1], col=col_of(m)).wait_recv()
    w_mid[...] = total(w_col, cols)
    for j in range(1, rows):
        start(w_mid.at[row_of(j)], w_row.at[me_r], wr_s.at[j - 1], wr_r.at[j - 1], row=row_of(j))
    w_row[me_r] = w_mid[me_r]

    def back_terms(k):
        for j in list(range(1, rows)) + [0]:
            q = row_of(j) * depths + deep_of(k)
            at = pl.ds(pl.multiple_of(q * nodes, nodes), nodes)
            term = jnp.dot(turned, block[:, at], preferred_element_type=f32)
            if j == 0:
                back_own[k] = term
            else:
                back_send[k, j - 1] = term.astype(bf16)
                start(
                    back_send.at[k, j - 1],
                    back_row.at[k, j - 1],
                    back_s.at[k, j - 1],
                    back_r.at[k, j - 1],
                    row=row_of(j),
                )

    back_order = deep_order + [0]
    back_terms(back_order[0])
    for j in range(1, rows):
        r = row_of(rows - j)
        send(w_mid.at[r], w_row.at[r], wr_s.at[j - 1], wr_r.at[j - 1], row=row_of(j)).wait_recv()
    w_deep[me_d] = total(w_row, rows)
    for k in range(1, depths):
        start(w_deep.at[me_d], w_deep.at[me_d], wd_s.at[k - 1], wd_r.at[k - 1], depth=deep_of(k))
    for k in back_order[1:]:
        back_terms(k)
    for k in range(1, depths):
        send(
            w_deep.at[me_d], w_deep.at[deep_of(depths - k)], wd_s.at[k - 1], wd_r.at[k - 1], depth=deep_of(k)
        ).wait_recv()
    w_total = total(w_deep, depths) * grad_norm
    w_out[me_c, me_r] = w_total[8:]
    bias_grad[...] = jnp.sum(w_total[:8], axis=0, keepdims=True)
    for j in range(1, rows):
        start(w_out.at[me_c, me_r], w_out.at[me_c, me_r], wg_s.at[j - 1], wg_r.at[j - 1], row=row_of(j))

    def row_sum(k):
        value = back_own[k]
        for j in range(1, rows):
            send(
                back_send.at[k, j - 1],
                back_row.at[k, j - 1],
                back_s.at[k, j - 1],
                back_r.at[k, j - 1],
                row=row_of(j),
            ).wait_recv()
            value = value + back_row[k, j - 1].astype(f32)
        return value

    for k in deep_order:
        deep_send[k - 1] = row_sum(k).astype(bf16)
        start(deep_send.at[k - 1], deep_recv.at[k - 1], deep_s.at[k - 1], deep_r.at[k - 1], depth=deep_of(k))

    back = row_sum(0)

    for j in range(1, rows):
        r = row_of(rows - j)
        send(w_out.at[me_c, r], w_out.at[me_c, r], wg_s.at[j - 1], wg_r.at[j - 1], row=row_of(j)).wait_recv()
    for m in range(1, cols):
        start(w_out.at[me_c], w_out.at[me_c], wo_s.at[m - 1], wo_r.at[m - 1], col=col_of(m))

    for k in range(1, depths):
        send(
            deep_send.at[k - 1], deep_recv.at[k - 1], deep_s.at[k - 1], deep_r.at[k - 1], depth=deep_of(k)
        ).wait_recv()
        back = back + deep_recv[k - 1].astype(f32)
    input_gradient[...] = (scale[...] * (back.T + grads[me_c].astype(f32))).astype(bf16)

    for m in range(1, cols):
        c = lax.rem(me_c + cols - m, cols)
        send(w_out.at[c], w_out.at[c], wo_s.at[m - 1], wo_r.at[m - 1], col=col_of(m)).wait_recv()
    for c in range(cols):
        for r in range(rows):
            first = (c * rows + r) * band
            weight_grad[first : first + band] = w_out[c, r]
    for copy in sent:
        copy.wait_send()


def finish_kernel(*refs):
    count = (len(refs) - 1) // 2
    sems = refs[-1]
    copies = [pltpu.make_async_copy(refs[i], refs[count + i], sems.at[i]) for i in range(count)]
    for copy in copies:
        copy.start()
    for copy in copies:
        copy.wait()


def finish(*arrays):
    anywhere = pl.BlockSpec(memory_space=pl.ANY)
    return pl.pallas_call(
        finish_kernel,
        out_shape=tuple(jax.ShapeDtypeStruct(a.shape, a.dtype) for a in arrays),
        in_specs=[anywhere] * len(arrays),
        out_specs=(anywhere,) * len(arrays),
        scratch_shapes=[pltpu.SemaphoreType.DMA((len(arrays),))],
    )(*arrays)


def run_layer(sizes, grad_norm, block, features, degree, weight, bias, cotangent):
    rows, cols, depths = sizes
    nodes, width = features.shape
    wide = weight.shape[1]
    band = width // (cols * rows)
    f32, bf16 = jnp.float32, jnp.bfloat16

    def dma(*shape):
        return [pltpu.SemaphoreType.DMA(shape)] * 2

    return pl.pallas_call(
        functools.partial(layer_kernel, sizes, grad_norm),
        out_shape=(
            jax.ShapeDtypeStruct((nodes, wide), bf16),
            jax.ShapeDtypeStruct((width, wide), f32),
            jax.ShapeDtypeStruct((1, wide), f32),
            jax.ShapeDtypeStruct((nodes, width), bf16),
        ),
        in_specs=[pl.BlockSpec(memory_space=pl.ANY)] + [pl.BlockSpec(memory_space=pltpu.VMEM)] * 5,
        out_specs=(pl.BlockSpec(memory_space=pltpu.VMEM),) * 4,
        scratch_shapes=[
            pltpu.VMEM(block.shape, bf16),
            pltpu.VMEM((nodes, width), f32),
            pltpu.VMEM((rows * depths, nodes, width), bf16),
            pltpu.VMEM((cols * nodes, width), f32),
            pltpu.VMEM((cols - 1, nodes, width), f32),
            pltpu.VMEM((cols, nodes, width), bf16),
            pltpu.VMEM((depths, width, nodes), f32),
            pltpu.VMEM((depths, rows - 1, width, nodes), bf16),
            pltpu.VMEM((depths, rows - 1, width, nodes), bf16),
            pltpu.VMEM((depths - 1, width, nodes), bf16),
            pltpu.VMEM((depths - 1, width, nodes), bf16),
            pltpu.VMEM((cols, rows, band + 8, wide), f32),
            pltpu.VMEM((cols, rows, band + 8, wide), f32),
            pltpu.VMEM((rows, band + 8, wide), f32),
            pltpu.VMEM((rows, band + 8, wide), f32),
            pltpu.VMEM((depths, band + 8, wide), f32),
            pltpu.VMEM((cols, rows, band, wide), f32),
            pltpu.SemaphoreType.DMA(()),
            pltpu.SemaphoreType.DMA((depths, rows)),
            pltpu.SemaphoreType.DMA((rows * depths,)),
            *dma(cols - 1),
            *dma(cols - 1),
            *dma(depths, rows - 1),
            *dma(depths - 1),
            *dma(cols - 1),
            *dma(rows - 1),
            *dma(depths - 1),
            *dma(rows - 1),
            *dma(cols - 1),
        ],
        compiler_params=pltpu.CompilerParams(
            collective_id=0, has_side_effects=True, vmem_limit_bytes=56 * 1024 * 1024
        ),
    )(block, features, degree, weight, bias, cotangent)


def local(features, degree, tiles, tile_rows, tile_cols, tile_count, weight, bias, cotangent):
    node_dev, feature_width = features.shape
    tile_size = tiles.shape[-1]
    slot_total = tiles.shape[3]
    sizes = tuple(lax.axis_size(name) for name in ("row", "col", "depth"))
    row_tiles = sizes[1] * node_dev // tile_size
    span = sizes[0] * sizes[2] * node_dev // tile_size
    grad_norm = (node_dev * sizes[0] * sizes[1] * sizes[2]) ** (-0.5)
    block = build_block(
        tiles.reshape(slot_total, tile_size, tile_size),
        tile_rows.reshape(slot_total),
        tile_cols.reshape(slot_total),
        tile_count.reshape(1),
        row_tiles,
        span,
    )
    results = run_layer(
        sizes, grad_norm, block, features, degree.reshape(1, -1), weight, bias.reshape(1, -1), cotangent
    )
    hidden, weight_grad, bias_grad, input_gradient = finish(*results)
    return (hidden, weight_grad, bias_grad.reshape(-1), input_gradient)


def solution(mesh):
    return jax.shard_map(
        local,
        mesh=mesh,
        in_specs=(
            P(("row", "col", "depth"), None),
            P(("row", "col", "depth")),
            P("row", "col", "depth", None, None, None),
            P("row", "col", "depth", None),
            P("row", "col", "depth", None),
            P("row", "col", "depth"),
            P(),
            P(),
            P(("row", "col", "depth"), None),
        ),
        out_specs=(P(("row", "col", "depth"), None), P(), P(), P(("row", "col", "depth"), None)),
        check_vma=False,
    )
```

```python
import functools

import jax
import jax.numpy as jnp
from jax import lax
from jax.experimental import pallas as pl
from jax.experimental.pallas import tpu as pltpu
from jax.sharding import PartitionSpec as P


def build_kernel(chunk, rows_ref, cols_ref, count_ref, tiles_ref, out_ref, held, sems):
    slots, tile, _ = held.shape
    live = count_ref[0]

    def fetch(k):
        part = pl.ds(k * chunk, chunk)
        return pltpu.make_async_copy(tiles_ref.at[part], held.at[part], sems.at[k])

    for k in range(slots // chunk):

        @pl.when(k * chunk < live)
        def _():
            fetch(k).start()

    zero = jnp.zeros((16, out_ref.shape[1]), out_ref.dtype)

    def clear(i, carry):
        out_ref[pl.ds(pl.multiple_of(i * 16, 16), 16), :] = zero
        return carry

    lax.fori_loop(0, out_ref.shape[0] // 16, clear, 0)

    def add(t, carry):
        at = (
            pl.ds(pl.multiple_of(rows_ref[t] * tile, tile), tile),
            pl.ds(pl.multiple_of(cols_ref[t] * tile, tile), tile),
        )
        out_ref[at] = out_ref[at] + held[t]
        return carry

    for k in range(slots // chunk):

        @pl.when(k * chunk < live)
        def _():
            fetch(k).wait()
            lax.fori_loop(k * chunk, jnp.minimum((k + 1) * chunk, live), add, 0)


def build_block(tiles, rows, cols, count, row_tiles, col_tiles):
    slots, tile, _ = tiles.shape
    chunk = 32
    shape = (row_tiles * tile, col_tiles * tile)
    smem = pl.BlockSpec(memory_space=pltpu.SMEM)
    return pl.pallas_call(
        functools.partial(build_kernel, chunk),
        out_shape=jax.ShapeDtypeStruct(shape, jnp.bfloat16),
        in_specs=[smem, smem, smem, pl.BlockSpec(memory_space=pl.ANY)],
        out_specs=pl.BlockSpec(memory_space=pltpu.VMEM),
        scratch_shapes=[
            pltpu.VMEM(tiles.shape, tiles.dtype),
            pltpu.SemaphoreType.DMA((slots // chunk,)),
        ],
        compiler_params=pltpu.CompilerParams(vmem_limit_bytes=56 * 1024 * 1024),
        cost_estimate=pl.CostEstimate(
            flops=tiles.size, bytes_accessed=tiles.size * 2 + shape[0] * shape[1] * 2, transcendentals=0
        ),
    )(rows, cols, count, tiles)


def silu_parts(pre_act):
    sigma = jax.nn.sigmoid(pre_act)
    return (pre_act * sigma, sigma * (1.0 + pre_act * (1.0 - sigma)))


def layer_kernel(
    sizes,
    grad_norm,
    block_hbm,
    features,
    degree,
    weight,
    bias,
    cotangent,
    hidden,
    weight_grad,
    bias_grad,
    input_gradient,
    block,
    scale,
    panel,
    acc,
    share,
    grads,
    back_own,
    back_send,
    back_row,
    deep_send,
    deep_recv,
    w_send,
    w_col,
    w_mid,
    w_row,
    w_deep,
    w_out,
    block_s,
    panel_s,
    panel_r,
    share_s,
    share_r,
    grads_s,
    grads_r,
    back_s,
    back_r,
    deep_s,
    deep_r,
    wc_s,
    wc_r,
    wr_s,
    wr_r,
    wd_s,
    wd_r,
    wg_s,
    wg_r,
    wo_s,
    wo_r,
):
    rows, cols, depths = sizes
    nodes = features.shape[0]
    me_r, me_c, me_d = (lax.axis_index(name) for name in ("row", "col", "depth"))
    f32, bf16 = jnp.float32, jnp.bfloat16

    def row_of(j):
        return lax.rem(me_r + j, rows)

    def col_of(m):
        return lax.rem(me_c + m, cols)

    def deep_of(k):
        return lax.rem(me_d + k, depths)

    def send(src, dst, send_sem, recv_sem, **peer):
        return pltpu.make_async_remote_copy(
            src_ref=src,
            dst_ref=dst,
            send_sem=send_sem,
            recv_sem=recv_sem,
            device_id=peer,
            device_id_type=pl.DeviceIdType.MESH,
        )

    sent = []

    def start(*args, **peer):
        copy = send(*args, **peer)
        copy.start()
        sent.append(copy)

    deep_order = sorted(range(1, depths), key=lambda k: (min(k, depths - k), k))

    bring = pltpu.make_async_copy(block_hbm, block, block_s)
    bring.start()
    barrier = pltpu.get_barrier_semaphore()
    for m in range(1, cols):
        pl.semaphore_signal(barrier, inc=1, device_id={"col": col_of(m)}, device_id_type=pl.DeviceIdType.MESH)
    for j in range(1, rows):
        pl.semaphore_signal(barrier, inc=1, device_id={"row": row_of(j)}, device_id_type=pl.DeviceIdType.MESH)
    for k in range(1, depths):
        pl.semaphore_signal(barrier, inc=1, device_id={"depth": deep_of(k)}, device_id_type=pl.DeviceIdType.MESH)
    mine = me_r * depths + me_d
    node_scale = lax.rsqrt(degree[...].astype(f32))
    scale[...] = jnp.broadcast_to(node_scale, features.shape[::-1]).T
    scaled = (features[...].astype(f32) * scale[...]).astype(bf16)
    panel[mine] = scaled
    pl.semaphore_wait(barrier, cols + rows + depths - 3)

    for k in deep_order:
        start(panel.at[mine], panel.at[mine], panel_s.at[k, 0], panel_r.at[mine], depth=deep_of(k))
    for j in range(1, rows):
        start(panel.at[mine], panel.at[mine], panel_s.at[0, j], panel_r.at[mine], row=row_of(j))

    def product(q):
        at = pl.ds(pl.multiple_of(q * nodes, nodes), nodes)
        return jnp.dot(block[:, at], panel[q], preferred_element_type=f32)

    bring.wait()
    acc[...] = product(mine)
    for k in deep_order:
        q = me_r * depths + deep_of(k)
        send(panel.at[q], panel.at[q], panel_s.at[k, 0], panel_r.at[q], depth=deep_of(k)).wait_recv()
        for j in range(1, rows):
            start(panel.at[q], panel.at[q], panel_s.at[k, j], panel_r.at[q], row=row_of(j))
        acc[...] += product(q)
    for k in [0] + deep_order:
        for j in range(1, rows):
            q = row_of(j) * depths + deep_of(k)
            send(panel.at[q], panel.at[q], panel_s.at[k, j], panel_r.at[q], row=row_of(j)).wait_recv()
            acc[...] += product(q)

    def acc_of(c):
        return acc.at[pl.ds(pl.multiple_of(c * nodes, nodes), nodes)]

    for m in range(1, cols):
        start(acc_of(col_of(m)), share.at[m - 1], share_s.at[m - 1], share_r.at[m - 1], col=col_of(m))
    aggregate = acc_of(me_c)[...]
    for m in range(1, cols):
        send(acc_of(me_c), share.at[m - 1], share_s.at[m - 1], share_r.at[m - 1], col=col_of(m)).wait_recv()
        aggregate = aggregate + share[m - 1]

    mixed = (scale[...] * (aggregate + scaled.astype(f32))).astype(bf16)
    pre_act = jnp.dot(mixed, weight[...], preferred_element_type=f32) + bias[...]
    activated, slope_value = silu_parts(pre_act)
    hidden[...] = activated.astype(bf16)
    pre_grad = (cotangent[...].astype(f32) * slope_value).astype(bf16)
    agg_grad = lax.dot_general(
        pre_grad, weight[...], (((1,), (1,)), ((), ())), preferred_element_type=f32
    ).astype(bf16)
    scaled_grad = (agg_grad.astype(f32) * scale[...]).astype(bf16)
    grads[me_c] = scaled_grad
    for m in range(1, cols):
        start(grads.at[me_c], grads.at[me_c], grads_s.at[m - 1], grads_r.at[m - 1], col=col_of(m))

    w_part = lax.dot_general(mixed, pre_grad, (((0,), (0,)), ((), ())), preferred_element_type=f32)
    b_part = jnp.sum(pre_grad.astype(f32).reshape(nodes // 8, 8, pre_grad.shape[1]), axis=0)
    band = w_part.shape[0] // (cols * rows)
    for c in range(cols):
        for r in range(rows):
            first = (c * rows + r) * band
            w_send[c, r, :8] = b_part
            w_send[c, r, 8:] = w_part[first : first + band]
    for m in range(1, cols):
        start(w_send.at[col_of(m)], w_col.at[me_c], wc_s.at[m - 1], wc_r.at[m - 1], col=col_of(m))
    w_col[me_c] = w_send[me_c]

    for m in range(1, cols):
        c = lax.rem(me_c + cols - m, cols)
        send(grads.at[c], grads.at[c], grads_s.at[m - 1], grads_r.at[m - 1], col=col_of(m)).wait_recv()
    turned = grads[...].reshape(cols * nodes, scaled_grad.shape[1]).T

    def total(buffer, count):
        value = buffer[0]
        for i in range(1, count):
            value = value + buffer[i]
        return value

    for m in range(1, cols):
        c = lax.rem(me_c + cols - m, cols)
        send(w_send.at[c], w_col.at[c], wc_s.at[m - 1], wc_r.at[m - 1], col=col_of(m)).wait_recv()
    w_mid[...] = total(w_col, cols)
    for j in range(1, rows):
        start(w_mid.at[row_of(j)], w_row.at[me_r], wr_s.at[j - 1], wr_r.at[j - 1], row=row_of(j))
    w_row[me_r] = w_mid[me_r]

    def back_terms(k):
        for j in list(range(1, rows)) + [0]:
            q = row_of(j) * depths + deep_of(k)
            at = pl.ds(pl.multiple_of(q * nodes, nodes), nodes)
            term = jnp.dot(turned, block[:, at], preferred_element_type=f32)
            if j == 0:
                back_own[k] = term
            else:
                back_send[k, j - 1] = term.astype(bf16)
                start(
                    back_send.at[k, j - 1],
                    back_row.at[k, j - 1],
                    back_s.at[k, j - 1],
                    back_r.at[k, j - 1],
                    row=row_of(j),
                )

    back_order = deep_order + [0]
    back_terms(back_order[0])
    for j in range(1, rows):
        r = row_of(rows - j)
        send(w_mid.at[r], w_row.at[r], wr_s.at[j - 1], wr_r.at[j - 1], row=row_of(j)).wait_recv()
    w_deep[me_d] = total(w_row, rows)
    for k in range(1, depths):
        start(w_deep.at[me_d], w_deep.at[me_d], wd_s.at[k - 1], wd_r.at[k - 1], depth=deep_of(k))
    for k in back_order[1:]:
        back_terms(k)
    for k in range(1, depths):
        send(
            w_deep.at[me_d], w_deep.at[deep_of(depths - k)], wd_s.at[k - 1], wd_r.at[k - 1], depth=deep_of(k)
        ).wait_recv()
    w_total = total(w_deep, depths) * grad_norm
    w_out[me_c, me_r] = w_total[8:]
    bias_grad[...] = jnp.sum(w_total[:8], axis=0, keepdims=True)
    for j in range(1, rows):
        start(w_out.at[me_c, me_r], w_out.at[me_c, me_r], wg_s.at[j - 1], wg_r.at[j - 1], row=row_of(j))

    def row_sum(k):
        value = back_own[k]
        for j in range(1, rows):
            send(
                back_send.at[k, j - 1],
                back_row.at[k, j - 1],
                back_s.at[k, j - 1],
                back_r.at[k, j - 1],
                row=row_of(j),
            ).wait_recv()
            value = value + back_row[k, j - 1].astype(f32)
        return value

    for k in deep_order:
        deep_send[k - 1] = row_sum(k).astype(bf16)
        start(deep_send.at[k - 1], deep_recv.at[k - 1], deep_s.at[k - 1], deep_r.at[k - 1], depth=deep_of(k))

    back = row_sum(0)

    for j in range(1, rows):
        r = row_of(rows - j)
        send(w_out.at[me_c, r], w_out.at[me_c, r], wg_s.at[j - 1], wg_r.at[j - 1], row=row_of(j)).wait_recv()
    for m in range(1, cols):
        start(w_out.at[me_c], w_out.at[me_c], wo_s.at[m - 1], wo_r.at[m - 1], col=col_of(m))

    for k in range(1, depths):
        send(
            deep_send.at[k - 1], deep_recv.at[k - 1], deep_s.at[k - 1], deep_r.at[k - 1], depth=deep_of(k)
        ).wait_recv()
        back = back + deep_recv[k - 1].astype(f32)
    input_gradient[...] = (scale[...] * (back.T + grads[me_c].astype(f32))).astype(bf16)

    for m in range(1, cols):
        c = lax.rem(me_c + cols - m, cols)
        send(w_out.at[c], w_out.at[c], wo_s.at[m - 1], wo_r.at[m - 1], col=col_of(m)).wait_recv()
    for c in range(cols):
        for r in range(rows):
            first = (c * rows + r) * band
            weight_grad[first : first + band] = w_out[c, r]
    for copy in sent:
        copy.wait_send()


def finish_kernel(*refs):
    count = len(refs) // 2
    for i in range(count):
        refs[count + i][...] = refs[i][...]


def finish(*arrays):
    vmem = pl.BlockSpec(memory_space=pltpu.VMEM)
    return pl.pallas_call(
        finish_kernel,
        out_shape=tuple(jax.ShapeDtypeStruct(a.shape, a.dtype) for a in arrays),
        in_specs=[vmem] * len(arrays),
        out_specs=(vmem,) * len(arrays),
    )(*arrays)


def run_layer(sizes, grad_norm, block, features, degree, weight, bias, cotangent):
    rows, cols, depths = sizes
    nodes, width = features.shape
    wide = weight.shape[1]
    band = width // (cols * rows)
    f32, bf16 = jnp.float32, jnp.bfloat16

    def dma(*shape):
        return [pltpu.SemaphoreType.DMA(shape)] * 2

    return pl.pallas_call(
        functools.partial(layer_kernel, sizes, grad_norm),
        out_shape=(
            jax.ShapeDtypeStruct((nodes, wide), bf16),
            jax.ShapeDtypeStruct((width, wide), f32),
            jax.ShapeDtypeStruct((1, wide), f32),
            jax.ShapeDtypeStruct((nodes, width), bf16),
        ),
        in_specs=[pl.BlockSpec(memory_space=pl.ANY)] + [pl.BlockSpec(memory_space=pltpu.VMEM)] * 5,
        out_specs=(pl.BlockSpec(memory_space=pltpu.VMEM),) * 4,
        scratch_shapes=[
            pltpu.VMEM(block.shape, bf16),
            pltpu.VMEM((nodes, width), f32),
            pltpu.VMEM((rows * depths, nodes, width), bf16),
            pltpu.VMEM((cols * nodes, width), f32),
            pltpu.VMEM((cols - 1, nodes, width), f32),
            pltpu.VMEM((cols, nodes, width), bf16),
            pltpu.VMEM((depths, width, nodes), f32),
            pltpu.VMEM((depths, rows - 1, width, nodes), bf16),
            pltpu.VMEM((depths, rows - 1, width, nodes), bf16),
            pltpu.VMEM((depths - 1, width, nodes), bf16),
            pltpu.VMEM((depths - 1, width, nodes), bf16),
            pltpu.VMEM((cols, rows, band + 8, wide), f32),
            pltpu.VMEM((cols, rows, band + 8, wide), f32),
            pltpu.VMEM((rows, band + 8, wide), f32),
            pltpu.VMEM((rows, band + 8, wide), f32),
            pltpu.VMEM((depths, band + 8, wide), f32),
            pltpu.VMEM((cols, rows, band, wide), f32),
            pltpu.SemaphoreType.DMA(()),
            pltpu.SemaphoreType.DMA((depths, rows)),
            pltpu.SemaphoreType.DMA((rows * depths,)),
            *dma(cols - 1),
            *dma(cols - 1),
            *dma(depths, rows - 1),
            *dma(depths - 1),
            *dma(cols - 1),
            *dma(rows - 1),
            *dma(depths - 1),
            *dma(rows - 1),
            *dma(cols - 1),
        ],
        compiler_params=pltpu.CompilerParams(
            collective_id=0, has_side_effects=True, vmem_limit_bytes=56 * 1024 * 1024
        ),
    )(block, features, degree, weight, bias, cotangent)


def local(features, degree, tiles, tile_rows, tile_cols, tile_count, weight, bias, cotangent):
    node_dev, feature_width = features.shape
    tile_size = tiles.shape[-1]
    slot_total = tiles.shape[3]
    sizes = tuple(lax.axis_size(name) for name in ("row", "col", "depth"))
    row_tiles = sizes[1] * node_dev // tile_size
    span = sizes[0] * sizes[2] * node_dev // tile_size
    grad_norm = (node_dev * sizes[0] * sizes[1] * sizes[2]) ** (-0.5)
    block = build_block(
        tiles.reshape(slot_total, tile_size, tile_size),
        tile_rows.reshape(slot_total),
        tile_cols.reshape(slot_total),
        tile_count.reshape(1),
        row_tiles,
        span,
    )
    results = run_layer(
        sizes, grad_norm, block, features, degree.reshape(1, -1), weight, bias.reshape(1, -1), cotangent
    )
    hidden, weight_grad, bias_grad, input_gradient = finish(*results)
    return (hidden, weight_grad, bias_grad.reshape(-1), input_gradient)


def solution(mesh):
    return jax.shard_map(
        local,
        mesh=mesh,
        in_specs=(
            P(("row", "col", "depth"), None),
            P(("row", "col", "depth")),
            P("row", "col", "depth", None, None, None),
            P("row", "col", "depth", None),
            P("row", "col", "depth", None),
            P("row", "col", "depth"),
            P(),
            P(),
            P(("row", "col", "depth"), None),
        ),
        out_specs=(P(("row", "col", "depth"), None), P(), P(), P(("row", "col", "depth"), None)),
        check_vma=False,
    )
```

```python
import functools

import jax
import jax.numpy as jnp
from jax import lax
from jax.experimental import pallas as pl
from jax.experimental.pallas import tpu as pltpu
from jax.sharding import PartitionSpec as P


def build_kernel(chunk, rows_ref, cols_ref, count_ref, tiles_ref, out_ref, held, sems):
    slots, tile, _ = held.shape
    live = count_ref[0]

    def fetch(k):
        part = pl.ds(k * chunk, chunk)
        return pltpu.make_async_copy(tiles_ref.at[part], held.at[part], sems.at[k])

    for k in range(slots // chunk):

        @pl.when(k * chunk < live)
        def _():
            fetch(k).start()

    zero = jnp.zeros((16, out_ref.shape[1]), out_ref.dtype)

    def clear(i, carry):
        out_ref[pl.ds(pl.multiple_of(i * 16, 16), 16), :] = zero
        return carry

    lax.fori_loop(0, out_ref.shape[0] // 16, clear, 0)

    def add(t, carry):
        at = (
            pl.ds(pl.multiple_of(rows_ref[t] * tile, tile), tile),
            pl.ds(pl.multiple_of(cols_ref[t] * tile, tile), tile),
        )
        out_ref[at] = out_ref[at] + held[t]
        return carry

    for k in range(slots // chunk):

        @pl.when(k * chunk < live)
        def _():
            fetch(k).wait()
            lax.fori_loop(k * chunk, jnp.minimum((k + 1) * chunk, live), add, 0)


def build_block(tiles, rows, cols, count, row_tiles, col_tiles):
    slots, tile, _ = tiles.shape
    chunk = 32
    shape = (row_tiles * tile, col_tiles * tile)
    smem = pl.BlockSpec(memory_space=pltpu.SMEM)
    return pl.pallas_call(
        functools.partial(build_kernel, chunk),
        out_shape=jax.ShapeDtypeStruct(shape, jnp.bfloat16),
        in_specs=[smem, smem, smem, pl.BlockSpec(memory_space=pl.ANY)],
        out_specs=pl.BlockSpec(memory_space=pltpu.VMEM),
        scratch_shapes=[
            pltpu.VMEM(tiles.shape, tiles.dtype),
            pltpu.SemaphoreType.DMA((slots // chunk,)),
        ],
        compiler_params=pltpu.CompilerParams(vmem_limit_bytes=56 * 1024 * 1024),
        cost_estimate=pl.CostEstimate(
            flops=tiles.size, bytes_accessed=tiles.size * 2 + shape[0] * shape[1] * 2, transcendentals=0
        ),
    )(rows, cols, count, tiles)


def silu_parts(pre_act):
    sigma = jax.nn.sigmoid(pre_act)
    return (pre_act * sigma, sigma * (1.0 + pre_act * (1.0 - sigma)))


def layer_kernel(
    sizes,
    grad_norm,
    block_hbm,
    features,
    degree,
    weight,
    bias,
    cotangent,
    hidden,
    weight_grad,
    bias_grad,
    input_gradient,
    block,
    scale,
    panel,
    acc,
    share,
    grads,
    back_own,
    back_held,
    back_send,
    back_row,
    deep_send,
    deep_recv,
    w_send,
    w_col,
    w_mid,
    w_row,
    w_deep,
    w_out,
    block_s,
    panel_s,
    panel_r,
    panel_f,
    panel_h,
    share_s,
    share_r,
    grads_s,
    grads_r,
    back_s,
    back_r,
    relay_s,
    relay_r,
    deep_s,
    deep_r,
    wc_s,
    wc_r,
    wr_s,
    wr_r,
    wd_s,
    wd_r,
    wg_s,
    wg_r,
    wo_s,
    wo_r,
):
    rows, cols, depths = sizes
    nodes = features.shape[0]
    me_r, me_c, me_d = (lax.axis_index(name) for name in ("row", "col", "depth"))
    f32, bf16 = jnp.float32, jnp.bfloat16

    corner = (me_r, me_r + 1 - 2 * lax.rem(me_r, 2), lax.rem(me_r + 2, 4), 3 - me_r)

    def row_of(j):
        return lax.rem(me_r + j, rows)

    def col_of(m):
        return lax.rem(me_c + m, cols)

    def deep_of(k):
        return lax.rem(me_d + k, depths)

    def send(src, dst, send_sem, recv_sem, **peer):
        return pltpu.make_async_remote_copy(
            src_ref=src,
            dst_ref=dst,
            send_sem=send_sem,
            recv_sem=recv_sem,
            device_id=peer,
            device_id_type=pl.DeviceIdType.MESH,
        )

    sent = []

    def start(*args, **peer):
        copy = send(*args, **peer)
        copy.start()
        sent.append(copy)

    deep_order = sorted(range(1, depths), key=lambda k: (min(k, depths - k), k))

    bring = pltpu.make_async_copy(block_hbm, block, block_s)
    bring.start()
    barrier = pltpu.get_barrier_semaphore()
    for m in range(1, cols):
        pl.semaphore_signal(barrier, inc=1, device_id={"col": col_of(m)}, device_id_type=pl.DeviceIdType.MESH)
    for j in range(1, rows):
        pl.semaphore_signal(barrier, inc=1, device_id={"row": row_of(j)}, device_id_type=pl.DeviceIdType.MESH)
    for k in range(1, depths):
        pl.semaphore_signal(barrier, inc=1, device_id={"depth": deep_of(k)}, device_id_type=pl.DeviceIdType.MESH)
    mine = me_r * depths + me_d
    node_scale = lax.rsqrt(degree[...].astype(f32))
    scale[...] = jnp.broadcast_to(node_scale, features.shape[::-1]).T
    scaled = (features[...].astype(f32) * scale[...]).astype(bf16)
    panel[mine] = scaled
    pl.semaphore_wait(barrier, cols + rows + depths - 3)

    for k in deep_order:
        start(panel.at[mine], panel.at[mine], panel_s.at[k, 0], panel_r.at[mine], depth=deep_of(k))
    for j in (1, 2):
        start(panel.at[mine], panel.at[mine], panel_s.at[0, j], panel_r.at[mine], row=corner[j])

    def product(q):
        at = pl.ds(pl.multiple_of(q * nodes, nodes), nodes)
        return jnp.dot(block[:, at], panel[q], preferred_element_type=f32)

    bring.wait()
    acc[...] = product(mine)
    half = nodes // 2

    def part(q, h):
        return panel.at[q, pl.ds(h * half, half)]

    def from_neighbours(k):
        for j in (1, 2):
            q = corner[j] * depths + deep_of(k)
            send(panel.at[q], panel.at[q], panel_s.at[k, j], panel_r.at[q], row=corner[j]).wait_recv()
            arrived = panel_r if j == 1 else panel_h
            start(part(q, j - 1), part(q, j - 1), panel_f.at[k, j - 1], arrived.at[q], row=corner[3 - j])
            acc[...] += product(q)

    order = [0] + deep_order
    for i, k in enumerate(deep_order):
        q = me_r * depths + deep_of(k)
        send(panel.at[q], panel.at[q], panel_s.at[k, 0], panel_r.at[q], depth=deep_of(k)).wait_recv()
        for j in (1, 2):
            start(panel.at[q], panel.at[q], panel_s.at[k, j], panel_r.at[q], row=corner[j])
        acc[...] += product(q)
        from_neighbours(order[i])
    from_neighbours(order[-1])
    for k in order:
        q = corner[3] * depths + deep_of(k)
        send(part(q, 0), part(q, 0), panel_f.at[k, 0], panel_r.at[q], row=corner[2]).wait_recv()
        send(part(q, 1), part(q, 1), panel_f.at[k, 1], panel_h.at[q], row=corner[1]).wait_recv()
        acc[...] += product(q)

    def acc_of(c):
        return acc.at[pl.ds(pl.multiple_of(c * nodes, nodes), nodes)]

    for m in range(1, cols):
        start(acc_of(col_of(m)), share.at[m - 1], share_s.at[m - 1], share_r.at[m - 1], col=col_of(m))
    aggregate = acc_of(me_c)[...]
    for m in range(1, cols):
        send(acc_of(me_c), share.at[m - 1], share_s.at[m - 1], share_r.at[m - 1], col=col_of(m)).wait_recv()
        aggregate = aggregate + share[m - 1]

    mixed = (scale[...] * (aggregate + scaled.astype(f32))).astype(bf16)
    pre_act = jnp.dot(mixed, weight[...], preferred_element_type=f32) + bias[...]
    activated, slope_value = silu_parts(pre_act)
    hidden[...] = activated.astype(bf16)
    pre_grad = (cotangent[...].astype(f32) * slope_value).astype(bf16)
    agg_grad = lax.dot_general(
        pre_grad, weight[...], (((1,), (1,)), ((), ())), preferred_element_type=f32
    ).astype(bf16)
    scaled_grad = (agg_grad.astype(f32) * scale[...]).astype(bf16)
    grads[me_c] = scaled_grad
    for m in range(1, cols):
        start(grads.at[me_c], grads.at[me_c], grads_s.at[m - 1], grads_r.at[m - 1], col=col_of(m))

    w_part = lax.dot_general(mixed, pre_grad, (((0,), (0,)), ((), ())), preferred_element_type=f32)
    b_part = jnp.sum(pre_grad.astype(f32).reshape(nodes // 8, 8, pre_grad.shape[1]), axis=0)
    band = w_part.shape[0] // (cols * rows)
    for c in range(cols):
        for r in range(rows):
            first = (c * rows + r) * band
            w_send[c, r, :8] = b_part
            w_send[c, r, 8:] = w_part[first : first + band]
    for m in range(1, cols):
        start(w_send.at[col_of(m)], w_col.at[me_c], wc_s.at[m - 1], wc_r.at[m - 1], col=col_of(m))
    w_col[me_c] = w_send[me_c]

    for m in range(1, cols):
        c = lax.rem(me_c + cols - m, cols)
        send(grads.at[c], grads.at[c], grads_s.at[m - 1], grads_r.at[m - 1], col=col_of(m)).wait_recv()
    turned = grads[...].reshape(cols * nodes, scaled_grad.shape[1]).T

    def total(buffer, count):
        value = buffer[0]
        for i in range(1, count):
            value = value + buffer[i]
        return value

    for m in range(1, cols):
        c = lax.rem(me_c + cols - m, cols)
        send(w_send.at[c], w_col.at[c], wc_s.at[m - 1], wc_r.at[m - 1], col=col_of(m)).wait_recv()
    w_mid[...] = total(w_col, cols)
    for j in range(1, rows):
        start(w_mid.at[row_of(j)], w_row.at[me_r], wr_s.at[j - 1], wr_r.at[j - 1], row=row_of(j))
    w_row[me_r] = w_mid[me_r]

    edge = features.shape[1] // 2

    def relay(k, h, peer):
        at = pl.ds(h * edge, edge)
        sems = (back_s.at[k, 2], back_r.at[k, 2]) if h == 0 else (relay_s.at[k], relay_r.at[k])
        return (back_send.at[k, 2, at], back_row.at[k, 2, at], *sems), {"row": corner[peer]}

    def back_terms(k):
        for j in (3, 1, 2, 0):
            q = corner[j] * depths + deep_of(k)
            at = pl.ds(pl.multiple_of(q * nodes, nodes), nodes)
            term = jnp.dot(turned, block[:, at], preferred_element_type=f32)
            if j == 0:
                back_own[k] = term
            elif j == 3:
                back_send[k, 2] = term.astype(bf16)
                for h in (0, 1):
                    args, peer = relay(k, h, h + 1)
                    start(*args, **peer)
            else:
                back_held[k, j - 1] = term

    def back_pass(k):
        for h in (0, 1):
            args, peer = relay(k, h, h + 1)
            send(*args, **peer).wait_recv()
        low, high = pl.ds(0, edge), pl.ds(edge, edge)
        back_send[k, 0, low] = back_held[k, 0, low].astype(bf16)
        back_send[k, 0, high] = (back_held[k, 0, high] + back_row[k, 2, high].astype(f32)).astype(bf16)
        back_send[k, 1, low] = (back_held[k, 1, low] + back_row[k, 2, low].astype(f32)).astype(bf16)
        back_send[k, 1, high] = back_held[k, 1, high].astype(bf16)
        for j in (1, 2):
            start(
                back_send.at[k, j - 1],
                back_row.at[k, j - 1],
                back_s.at[k, j - 1],
                back_r.at[k, j - 1],
                row=corner[j],
            )

    back_order = deep_order + [0]
    back_terms(back_order[0])
    back_terms(back_order[1])
    back_pass(back_order[0])
    for j in range(1, rows):
        r = row_of(rows - j)
        send(w_mid.at[r], w_row.at[r], wr_s.at[j - 1], wr_r.at[j - 1], row=row_of(j)).wait_recv()
    w_deep[me_d] = total(w_row, rows)
    for k in range(1, depths):
        start(w_deep.at[me_d], w_deep.at[me_d], wd_s.at[k - 1], wd_r.at[k - 1], depth=deep_of(k))
    for i in range(1, depths):
        if i + 1 < depths:
            back_terms(back_order[i + 1])
        back_pass(back_order[i])
    for k in range(1, depths):
        send(
            w_deep.at[me_d], w_deep.at[deep_of(depths - k)], wd_s.at[k - 1], wd_r.at[k - 1], depth=deep_of(k)
        ).wait_recv()
    w_total = total(w_deep, depths) * grad_norm
    w_out[me_c, me_r] = w_total[8:]
    bias_grad[...] = jnp.sum(w_total[:8], axis=0, keepdims=True)
    for j in range(1, rows):
        start(w_out.at[me_c, me_r], w_out.at[me_c, me_r], wg_s.at[j - 1], wg_r.at[j - 1], row=row_of(j))

    def row_sum(k):
        value = back_own[k]
        for j in (1, 2):
            send(
                back_send.at[k, j - 1],
                back_row.at[k, j - 1],
                back_s.at[k, j - 1],
                back_r.at[k, j - 1],
                row=corner[j],
            ).wait_recv()
            value = value + back_row[k, j - 1].astype(f32)
        return value

    for k in deep_order:
        deep_send[k - 1] = row_sum(k).astype(bf16)
        start(deep_send.at[k - 1], deep_recv.at[k - 1], deep_s.at[k - 1], deep_r.at[k - 1], depth=deep_of(k))

    back = row_sum(0)

    for j in range(1, rows):
        r = row_of(rows - j)
        send(w_out.at[me_c, r], w_out.at[me_c, r], wg_s.at[j - 1], wg_r.at[j - 1], row=row_of(j)).wait_recv()
    for m in range(1, cols):
        start(w_out.at[me_c], w_out.at[me_c], wo_s.at[m - 1], wo_r.at[m - 1], col=col_of(m))

    for k in range(1, depths):
        send(
            deep_send.at[k - 1], deep_recv.at[k - 1], deep_s.at[k - 1], deep_r.at[k - 1], depth=deep_of(k)
        ).wait_recv()
        back = back + deep_recv[k - 1].astype(f32)
    input_gradient[...] = (scale[...] * (back.T + grads[me_c].astype(f32))).astype(bf16)

    for m in range(1, cols):
        c = lax.rem(me_c + cols - m, cols)
        send(w_out.at[c], w_out.at[c], wo_s.at[m - 1], wo_r.at[m - 1], col=col_of(m)).wait_recv()
    for c in range(cols):
        for r in range(rows):
            first = (c * rows + r) * band
            weight_grad[first : first + band] = w_out[c, r]
    for copy in sent:
        copy.wait_send()


def finish_kernel(*refs):
    count = len(refs) // 2
    for i in range(count):
        refs[count + i][...] = refs[i][...]


def finish(*arrays):
    vmem = pl.BlockSpec(memory_space=pltpu.VMEM)
    return pl.pallas_call(
        finish_kernel,
        out_shape=tuple(jax.ShapeDtypeStruct(a.shape, a.dtype) for a in arrays),
        in_specs=[vmem] * len(arrays),
        out_specs=(vmem,) * len(arrays),
    )(*arrays)


def run_layer(sizes, grad_norm, block, features, degree, weight, bias, cotangent):
    rows, cols, depths = sizes
    nodes, width = features.shape
    wide = weight.shape[1]
    band = width // (cols * rows)
    f32, bf16 = jnp.float32, jnp.bfloat16

    def dma(*shape):
        return [pltpu.SemaphoreType.DMA(shape)] * 2

    return pl.pallas_call(
        functools.partial(layer_kernel, sizes, grad_norm),
        out_shape=(
            jax.ShapeDtypeStruct((nodes, wide), bf16),
            jax.ShapeDtypeStruct((width, wide), f32),
            jax.ShapeDtypeStruct((1, wide), f32),
            jax.ShapeDtypeStruct((nodes, width), bf16),
        ),
        in_specs=[pl.BlockSpec(memory_space=pl.ANY)] + [pl.BlockSpec(memory_space=pltpu.VMEM)] * 5,
        out_specs=(pl.BlockSpec(memory_space=pltpu.VMEM),) * 4,
        scratch_shapes=[
            pltpu.VMEM(block.shape, bf16),
            pltpu.VMEM((nodes, width), f32),
            pltpu.VMEM((rows * depths, nodes, width), bf16),
            pltpu.VMEM((cols * nodes, width), f32),
            pltpu.VMEM((cols - 1, nodes, width), f32),
            pltpu.VMEM((cols, nodes, width), bf16),
            pltpu.VMEM((depths, width, nodes), f32),
            pltpu.VMEM((depths, 2, width, nodes), f32),
            pltpu.VMEM((depths, rows - 1, width, nodes), bf16),
            pltpu.VMEM((depths, rows - 1, width, nodes), bf16),
            pltpu.VMEM((depths - 1, width, nodes), bf16),
            pltpu.VMEM((depths - 1, width, nodes), bf16),
            pltpu.VMEM((cols, rows, band + 8, wide), f32),
            pltpu.VMEM((cols, rows, band + 8, wide), f32),
            pltpu.VMEM((rows, band + 8, wide), f32),
            pltpu.VMEM((rows, band + 8, wide), f32),
            pltpu.VMEM((depths, band + 8, wide), f32),
            pltpu.VMEM((cols, rows, band, wide), f32),
            pltpu.SemaphoreType.DMA(()),
            pltpu.SemaphoreType.DMA((depths, rows)),
            pltpu.SemaphoreType.DMA((rows * depths,)),
            pltpu.SemaphoreType.DMA((depths, 2)),
            pltpu.SemaphoreType.DMA((rows * depths,)),
            *dma(cols - 1),
            *dma(cols - 1),
            *dma(depths, rows - 1),
            *dma(depths),
            *dma(depths - 1),
            *dma(cols - 1),
            *dma(rows - 1),
            *dma(depths - 1),
            *dma(rows - 1),
            *dma(cols - 1),
        ],
        compiler_params=pltpu.CompilerParams(
            collective_id=0, has_side_effects=True, vmem_limit_bytes=56 * 1024 * 1024
        ),
    )(block, features, degree, weight, bias, cotangent)


def local(features, degree, tiles, tile_rows, tile_cols, tile_count, weight, bias, cotangent):
    node_dev, feature_width = features.shape
    tile_size = tiles.shape[-1]
    slot_total = tiles.shape[3]
    sizes = tuple(lax.axis_size(name) for name in ("row", "col", "depth"))
    row_tiles = sizes[1] * node_dev // tile_size
    span = sizes[0] * sizes[2] * node_dev // tile_size
    grad_norm = (node_dev * sizes[0] * sizes[1] * sizes[2]) ** (-0.5)
    block = build_block(
        tiles.reshape(slot_total, tile_size, tile_size),
        tile_rows.reshape(slot_total),
        tile_cols.reshape(slot_total),
        tile_count.reshape(1),
        row_tiles,
        span,
    )
    results = run_layer(
        sizes, grad_norm, block, features, degree.reshape(1, -1), weight, bias.reshape(1, -1), cotangent
    )
    hidden, weight_grad, bias_grad, input_gradient = finish(*results)
    return (hidden, weight_grad, bias_grad.reshape(-1), input_gradient)


def solution(mesh):
    return jax.shard_map(
        local,
        mesh=mesh,
        in_specs=(
            P(("row", "col", "depth"), None),
            P(("row", "col", "depth")),
            P("row", "col", "depth", None, None, None),
            P("row", "col", "depth", None),
            P("row", "col", "depth", None),
            P("row", "col", "depth"),
            P(),
            P(),
            P(("row", "col", "depth"), None),
        ),
        out_specs=(P(("row", "col", "depth"), None), P(), P(), P(("row", "col", "depth"), None)),
        check_vma=False,
    )
```

```python
import functools

import jax
import jax.numpy as jnp
from jax import lax
from jax.experimental import pallas as pl
from jax.experimental.pallas import tpu as pltpu
from jax.sharding import PartitionSpec as P


def build_kernel(chunk, rows_ref, cols_ref, count_ref, tiles_ref, out_ref, held, sems):
    slots, tile, _ = held.shape
    live = count_ref[0]

    def fetch(k):
        part = pl.ds(k * chunk, chunk)
        return pltpu.make_async_copy(tiles_ref.at[part], held.at[part], sems.at[k])

    for k in range(slots // chunk):

        @pl.when(k * chunk < live)
        def _():
            fetch(k).start()

    zero = jnp.zeros((16, out_ref.shape[1]), out_ref.dtype)

    def clear(i, carry):
        out_ref[pl.ds(pl.multiple_of(i * 16, 16), 16), :] = zero
        return carry

    lax.fori_loop(0, out_ref.shape[0] // 16, clear, 0)

    def add(t, carry):
        at = (
            pl.ds(pl.multiple_of(rows_ref[t] * tile, tile), tile),
            pl.ds(pl.multiple_of(cols_ref[t] * tile, tile), tile),
        )
        out_ref[at] = out_ref[at] + held[t]
        return carry

    for k in range(slots // chunk):

        @pl.when(k * chunk < live)
        def _():
            fetch(k).wait()

        @pl.when((k + 1) * chunk <= live)
        def _():
            lax.fori_loop(k * chunk, (k + 1) * chunk, add, 0, unroll=8)

        @pl.when(((k + 1) * chunk > live) & (k * chunk < live))
        def _():
            lax.fori_loop(k * chunk, live, add, 0)


def build_block(tiles, rows, cols, count, row_tiles, col_tiles):
    slots, tile, _ = tiles.shape
    chunk = 32
    shape = (row_tiles * tile, col_tiles * tile)
    smem = pl.BlockSpec(memory_space=pltpu.SMEM)
    return pl.pallas_call(
        functools.partial(build_kernel, chunk),
        out_shape=jax.ShapeDtypeStruct(shape, jnp.bfloat16),
        in_specs=[smem, smem, smem, pl.BlockSpec(memory_space=pl.ANY)],
        out_specs=pl.BlockSpec(memory_space=pltpu.VMEM),
        scratch_shapes=[
            pltpu.VMEM(tiles.shape, tiles.dtype),
            pltpu.SemaphoreType.DMA((slots // chunk,)),
        ],
        compiler_params=pltpu.CompilerParams(vmem_limit_bytes=56 * 1024 * 1024),
        cost_estimate=pl.CostEstimate(
            flops=tiles.size, bytes_accessed=tiles.size * 2 + shape[0] * shape[1] * 2, transcendentals=0
        ),
    )(rows, cols, count, tiles)


def silu_parts(pre_act):
    sigma = jax.nn.sigmoid(pre_act)
    return (pre_act * sigma, sigma * (1.0 + pre_act * (1.0 - sigma)))


def layer_kernel(
    sizes,
    grad_norm,
    block_hbm,
    features,
    degree,
    weight,
    bias,
    cotangent,
    hidden,
    weight_grad,
    bias_grad,
    input_gradient,
    block,
    scale,
    panel,
    acc,
    share,
    grads,
    back_own,
    back_send,
    back_row,
    deep_send,
    deep_recv,
    w_send,
    w_col,
    w_mid,
    w_row,
    w_deep,
    w_out,
    block_s,
    panel_s,
    panel_r,
    share_s,
    share_r,
    grads_s,
    grads_r,
    back_s,
    back_r,
    deep_s,
    deep_r,
    wc_s,
    wc_r,
    wr_s,
    wr_r,
    wd_s,
    wd_r,
    wg_s,
    wg_r,
    wo_s,
    wo_r,
):
    rows, cols, depths = sizes
    nodes = features.shape[0]
    me_r, me_c, me_d = (lax.axis_index(name) for name in ("row", "col", "depth"))
    f32, bf16 = jnp.float32, jnp.bfloat16

    def row_of(j):
        return lax.rem(me_r + j, rows)

    def col_of(m):
        return lax.rem(me_c + m, cols)

    def deep_of(k):
        return lax.rem(me_d + k, depths)

    def send(src, dst, send_sem, recv_sem, **peer):
        return pltpu.make_async_remote_copy(
            src_ref=src,
            dst_ref=dst,
            send_sem=send_sem,
            recv_sem=recv_sem,
            device_id=peer,
            device_id_type=pl.DeviceIdType.MESH,
        )

    sent = []

    def start(*args, **peer):
        copy = send(*args, **peer)
        copy.start()
        sent.append(copy)

    deep_order = sorted(range(1, depths), key=lambda k: (min(k, depths - k), k))

    bring = pltpu.make_async_copy(block_hbm, block, block_s)
    bring.start()
    barrier = pltpu.get_barrier_semaphore()
    for m in range(1, cols):
        pl.semaphore_signal(barrier, inc=1, device_id={"col": col_of(m)}, device_id_type=pl.DeviceIdType.MESH)
    for j in range(1, rows):
        pl.semaphore_signal(barrier, inc=1, device_id={"row": row_of(j)}, device_id_type=pl.DeviceIdType.MESH)
    for k in range(1, depths):
        pl.semaphore_signal(barrier, inc=1, device_id={"depth": deep_of(k)}, device_id_type=pl.DeviceIdType.MESH)
    mine = me_r * depths + me_d
    node_scale = lax.rsqrt(degree[...].astype(f32))
    scale[...] = jnp.broadcast_to(node_scale, features.shape[::-1]).T
    scaled = (features[...].astype(f32) * scale[...]).astype(bf16)
    panel[mine] = scaled
    pl.semaphore_wait(barrier, cols + rows + depths - 3)

    for k in deep_order:
        start(panel.at[mine], panel.at[mine], panel_s.at[k, 0], panel_r.at[mine], depth=deep_of(k))
    for j in range(1, rows):
        start(panel.at[mine], panel.at[mine], panel_s.at[0, j], panel_r.at[mine], row=row_of(j))

    def product(q):
        at = pl.ds(pl.multiple_of(q * nodes, nodes), nodes)
        return jnp.dot(block[:, at], panel[q], preferred_element_type=f32)

    bring.wait()
    acc[...] = product(mine)
    for k in deep_order:
        q = me_r * depths + deep_of(k)
        send(panel.at[q], panel.at[q], panel_s.at[k, 0], panel_r.at[q], depth=deep_of(k)).wait_recv()
        for j in range(1, rows):
            start(panel.at[q], panel.at[q], panel_s.at[k, j], panel_r.at[q], row=row_of(j))
        acc[...] += product(q)
    for k in [0] + deep_order:
        for j in range(1, rows):
            q = row_of(j) * depths + deep_of(k)
            send(panel.at[q], panel.at[q], panel_s.at[k, j], panel_r.at[q], row=row_of(j)).wait_recv()
            acc[...] += product(q)

    def acc_of(c):
        return acc.at[pl.ds(pl.multiple_of(c * nodes, nodes), nodes)]

    for m in range(1, cols):
        start(acc_of(col_of(m)), share.at[m - 1], share_s.at[m - 1], share_r.at[m - 1], col=col_of(m))
    aggregate = acc_of(me_c)[...]
    for m in range(1, cols):
        send(acc_of(me_c), share.at[m - 1], share_s.at[m - 1], share_r.at[m - 1], col=col_of(m)).wait_recv()
        aggregate = aggregate + share[m - 1]

    mixed = (scale[...] * (aggregate + scaled.astype(f32))).astype(bf16)
    pre_act = jnp.dot(mixed, weight[...], preferred_element_type=f32) + bias[...]
    activated, slope_value = silu_parts(pre_act)
    hidden[...] = activated.astype(bf16)
    pre_grad = (cotangent[...].astype(f32) * slope_value).astype(bf16)
    agg_grad = lax.dot_general(
        pre_grad, weight[...], (((1,), (1,)), ((), ())), preferred_element_type=f32
    ).astype(bf16)
    scaled_grad = (agg_grad.astype(f32) * scale[...]).astype(bf16)
    grads[me_c] = scaled_grad
    for m in range(1, cols):
        start(grads.at[me_c], grads.at[me_c], grads_s.at[m - 1], grads_r.at[m - 1], col=col_of(m))

    w_part = lax.dot_general(mixed, pre_grad, (((0,), (0,)), ((), ())), preferred_element_type=f32)
    b_part = jnp.sum(pre_grad.astype(f32).reshape(nodes // 8, 8, pre_grad.shape[1]), axis=0)
    band = w_part.shape[0] // (cols * rows)
    for c in range(cols):
        for r in range(rows):
            first = (c * rows + r) * band
            w_send[c, r, :8] = b_part
            w_send[c, r, 8:] = w_part[first : first + band]
    for m in range(1, cols):
        start(w_send.at[col_of(m)], w_col.at[me_c], wc_s.at[m - 1], wc_r.at[m - 1], col=col_of(m))
    w_col[me_c] = w_send[me_c]

    for m in range(1, cols):
        c = lax.rem(me_c + cols - m, cols)
        send(grads.at[c], grads.at[c], grads_s.at[m - 1], grads_r.at[m - 1], col=col_of(m)).wait_recv()
    turned = grads[...].reshape(cols * nodes, scaled_grad.shape[1]).T

    def total(buffer, count):
        value = buffer[0]
        for i in range(1, count):
            value = value + buffer[i]
        return value

    for m in range(1, cols):
        c = lax.rem(me_c + cols - m, cols)
        send(w_send.at[c], w_col.at[c], wc_s.at[m - 1], wc_r.at[m - 1], col=col_of(m)).wait_recv()
    w_mid[...] = total(w_col, cols)
    for j in range(1, rows):
        start(w_mid.at[row_of(j)], w_row.at[me_r], wr_s.at[j - 1], wr_r.at[j - 1], row=row_of(j))
    w_row[me_r] = w_mid[me_r]

    def back_terms(k):
        for j in list(range(1, rows)) + [0]:
            q = row_of(j) * depths + deep_of(k)
            at = pl.ds(pl.multiple_of(q * nodes, nodes), nodes)
            term = jnp.dot(turned, block[:, at], preferred_element_type=f32)
            if j == 0:
                back_own[k] = term
            else:
                back_send[k, j - 1] = term.astype(bf16)
                start(
                    back_send.at[k, j - 1],
                    back_row.at[k, j - 1],
                    back_s.at[k, j - 1],
                    back_r.at[k, j - 1],
                    row=row_of(j),
                )

    back_order = deep_order + [0]
    back_terms(back_order[0])
    for j in range(1, rows):
        r = row_of(rows - j)
        send(w_mid.at[r], w_row.at[r], wr_s.at[j - 1], wr_r.at[j - 1], row=row_of(j)).wait_recv()
    w_deep[me_d] = total(w_row, rows)
    for k in range(1, depths):
        start(w_deep.at[me_d], w_deep.at[me_d], wd_s.at[k - 1], wd_r.at[k - 1], depth=deep_of(k))
    for k in back_order[1:]:
        back_terms(k)
    for k in range(1, depths):
        send(
            w_deep.at[me_d], w_deep.at[deep_of(depths - k)], wd_s.at[k - 1], wd_r.at[k - 1], depth=deep_of(k)
        ).wait_recv()
    w_total = total(w_deep, depths) * grad_norm
    w_out[me_c, me_r] = w_total[8:]
    bias_grad[...] = jnp.sum(w_total[:8], axis=0, keepdims=True)
    for j in range(1, rows):
        start(w_out.at[me_c, me_r], w_out.at[me_c, me_r], wg_s.at[j - 1], wg_r.at[j - 1], row=row_of(j))

    def row_sum(k):
        value = back_own[k]
        for j in range(1, rows):
            send(
                back_send.at[k, j - 1],
                back_row.at[k, j - 1],
                back_s.at[k, j - 1],
                back_r.at[k, j - 1],
                row=row_of(j),
            ).wait_recv()
            value = value + back_row[k, j - 1].astype(f32)
        return value

    for k in deep_order:
        deep_send[k - 1] = row_sum(k).astype(bf16)
        start(deep_send.at[k - 1], deep_recv.at[k - 1], deep_s.at[k - 1], deep_r.at[k - 1], depth=deep_of(k))

    back = row_sum(0)

    for j in range(1, rows):
        r = row_of(rows - j)
        send(w_out.at[me_c, r], w_out.at[me_c, r], wg_s.at[j - 1], wg_r.at[j - 1], row=row_of(j)).wait_recv()
    for m in range(1, cols):
        start(w_out.at[me_c], w_out.at[me_c], wo_s.at[m - 1], wo_r.at[m - 1], col=col_of(m))

    for k in range(1, depths):
        send(
            deep_send.at[k - 1], deep_recv.at[k - 1], deep_s.at[k - 1], deep_r.at[k - 1], depth=deep_of(k)
        ).wait_recv()
        back = back + deep_recv[k - 1].astype(f32)
    input_gradient[...] = (scale[...] * (back.T + grads[me_c].astype(f32))).astype(bf16)

    for m in range(1, cols):
        c = lax.rem(me_c + cols - m, cols)
        send(w_out.at[c], w_out.at[c], wo_s.at[m - 1], wo_r.at[m - 1], col=col_of(m)).wait_recv()
    for c in range(cols):
        for r in range(rows):
            first = (c * rows + r) * band
            weight_grad[first : first + band] = w_out[c, r]
    for copy in sent:
        copy.wait_send()


def finish_kernel(*refs):
    count = len(refs) // 2
    for i in range(count):
        refs[count + i][...] = refs[i][...]


def finish(*arrays):
    vmem = pl.BlockSpec(memory_space=pltpu.VMEM)
    return pl.pallas_call(
        finish_kernel,
        out_shape=tuple(jax.ShapeDtypeStruct(a.shape, a.dtype) for a in arrays),
        in_specs=[vmem] * len(arrays),
        out_specs=(vmem,) * len(arrays),
    )(*arrays)


def run_layer(sizes, grad_norm, block, features, degree, weight, bias, cotangent):
    rows, cols, depths = sizes
    nodes, width = features.shape
    wide = weight.shape[1]
    band = width // (cols * rows)
    f32, bf16 = jnp.float32, jnp.bfloat16

    def dma(*shape):
        return [pltpu.SemaphoreType.DMA(shape)] * 2

    return pl.pallas_call(
        functools.partial(layer_kernel, sizes, grad_norm),
        out_shape=(
            jax.ShapeDtypeStruct((nodes, wide), bf16),
            jax.ShapeDtypeStruct((width, wide), f32),
            jax.ShapeDtypeStruct((1, wide), f32),
            jax.ShapeDtypeStruct((nodes, width), bf16),
        ),
        in_specs=[pl.BlockSpec(memory_space=pl.ANY)] + [pl.BlockSpec(memory_space=pltpu.VMEM)] * 5,
        out_specs=(pl.BlockSpec(memory_space=pltpu.VMEM),) * 4,
        scratch_shapes=[
            pltpu.VMEM(block.shape, bf16),
            pltpu.VMEM((nodes, width), f32),
            pltpu.VMEM((rows * depths, nodes, width), bf16),
            pltpu.VMEM((cols * nodes, width), f32),
            pltpu.VMEM((cols - 1, nodes, width), f32),
            pltpu.VMEM((cols, nodes, width), bf16),
            pltpu.VMEM((depths, width, nodes), f32),
            pltpu.VMEM((depths, rows - 1, width, nodes), bf16),
            pltpu.VMEM((depths, rows - 1, width, nodes), bf16),
            pltpu.VMEM((depths - 1, width, nodes), bf16),
            pltpu.VMEM((depths - 1, width, nodes), bf16),
            pltpu.VMEM((cols, rows, band + 8, wide), f32),
            pltpu.VMEM((cols, rows, band + 8, wide), f32),
            pltpu.VMEM((rows, band + 8, wide), f32),
            pltpu.VMEM((rows, band + 8, wide), f32),
            pltpu.VMEM((depths, band + 8, wide), f32),
            pltpu.VMEM((cols, rows, band, wide), f32),
            pltpu.SemaphoreType.DMA(()),
            pltpu.SemaphoreType.DMA((depths, rows)),
            pltpu.SemaphoreType.DMA((rows * depths,)),
            *dma(cols - 1),
            *dma(cols - 1),
            *dma(depths, rows - 1),
            *dma(depths - 1),
            *dma(cols - 1),
            *dma(rows - 1),
            *dma(depths - 1),
            *dma(rows - 1),
            *dma(cols - 1),
        ],
        compiler_params=pltpu.CompilerParams(
            collective_id=0, has_side_effects=True, vmem_limit_bytes=56 * 1024 * 1024
        ),
    )(block, features, degree, weight, bias, cotangent)


def local(features, degree, tiles, tile_rows, tile_cols, tile_count, weight, bias, cotangent):
    node_dev, feature_width = features.shape
    tile_size = tiles.shape[-1]
    slot_total = tiles.shape[3]
    sizes = tuple(lax.axis_size(name) for name in ("row", "col", "depth"))
    row_tiles = sizes[1] * node_dev // tile_size
    span = sizes[0] * sizes[2] * node_dev // tile_size
    grad_norm = (node_dev * sizes[0] * sizes[1] * sizes[2]) ** (-0.5)
    block = build_block(
        tiles.reshape(slot_total, tile_size, tile_size),
        tile_rows.reshape(slot_total),
        tile_cols.reshape(slot_total),
        tile_count.reshape(1),
        row_tiles,
        span,
    )
    results = run_layer(
        sizes, grad_norm, block, features, degree.reshape(1, -1), weight, bias.reshape(1, -1), cotangent
    )
    hidden, weight_grad, bias_grad, input_gradient = finish(*results)
    return (hidden, weight_grad, bias_grad.reshape(-1), input_gradient)


def solution(mesh):
    return jax.shard_map(
        local,
        mesh=mesh,
        in_specs=(
            P(("row", "col", "depth"), None),
            P(("row", "col", "depth")),
            P("row", "col", "depth", None, None, None),
            P("row", "col", "depth", None),
            P("row", "col", "depth", None),
            P("row", "col", "depth"),
            P(),
            P(),
            P(("row", "col", "depth"), None),
        ),
        out_specs=(P(("row", "col", "depth"), None), P(), P(), P(("row", "col", "depth"), None)),
        check_vma=False,
    )
```

```python
import functools

import jax
import jax.numpy as jnp
from jax import lax
from jax.experimental import pallas as pl
from jax.experimental.pallas import tpu as pltpu
from jax.sharding import PartitionSpec as P


def build_kernel(chunk, rows_ref, cols_ref, count_ref, tiles_ref, out_ref, held, sems):
    slots, tile, _ = held.shape
    live = count_ref[0]

    def fetch(k):
        part = pl.ds(k * chunk, chunk)
        return pltpu.make_async_copy(tiles_ref.at[part], held.at[part], sems.at[k])

    for k in range(slots // chunk):

        @pl.when(k * chunk < live)
        def _():
            fetch(k).start()

    zero = jnp.zeros((16, out_ref.shape[1]), out_ref.dtype)

    def clear(i, carry):
        out_ref[pl.ds(pl.multiple_of(i * 16, 16), 16), :] = zero
        return carry

    lax.fori_loop(0, out_ref.shape[0] // 16, clear, 0)

    def place(t):
        return (
            pl.ds(pl.multiple_of(rows_ref[t] * tile, tile), tile),
            pl.ds(pl.multiple_of(cols_ref[t] * tile, tile), tile),
        )

    def add(t, carry):
        out_ref[place(t)] = out_ref[place(t)] + held[t]
        return carry

    def add_pair(i, carry):
        t, u = 2 * i, 2 * i + 1
        same = (rows_ref[t] == rows_ref[u]) & (cols_ref[t] == cols_ref[u])
        one, two = out_ref[place(t)], out_ref[place(u)]
        one = one + held[t]
        out_ref[place(t)] = one
        out_ref[place(u)] = jnp.where(same, one, two) + held[u]
        return carry

    for k in range(slots // chunk):

        @pl.when(k * chunk < live)
        def _():
            fetch(k).wait()

        @pl.when((k + 1) * chunk <= live)
        def _():
            lax.fori_loop(k * chunk // 2, (k + 1) * chunk // 2, add_pair, 0, unroll=4)

        @pl.when(((k + 1) * chunk > live) & (k * chunk < live))
        def _():
            lax.fori_loop(k * chunk, live, add, 0)


def build_block(tiles, rows, cols, count, row_tiles, col_tiles):
    slots, tile, _ = tiles.shape
    chunk = 32
    shape = (row_tiles * tile, col_tiles * tile)
    smem = pl.BlockSpec(memory_space=pltpu.SMEM)
    return pl.pallas_call(
        functools.partial(build_kernel, chunk),
        out_shape=jax.ShapeDtypeStruct(shape, jnp.bfloat16),
        in_specs=[smem, smem, smem, pl.BlockSpec(memory_space=pl.ANY)],
        out_specs=pl.BlockSpec(memory_space=pltpu.VMEM),
        scratch_shapes=[
            pltpu.VMEM(tiles.shape, tiles.dtype),
            pltpu.SemaphoreType.DMA((slots // chunk,)),
        ],
        compiler_params=pltpu.CompilerParams(vmem_limit_bytes=56 * 1024 * 1024),
        cost_estimate=pl.CostEstimate(
            flops=tiles.size, bytes_accessed=tiles.size * 2 + shape[0] * shape[1] * 2, transcendentals=0
        ),
    )(rows, cols, count, tiles)


def silu_parts(pre_act):
    sigma = jax.nn.sigmoid(pre_act)
    return (pre_act * sigma, sigma * (1.0 + pre_act * (1.0 - sigma)))


def layer_kernel(
    sizes,
    grad_norm,
    block_hbm,
    features,
    degree,
    weight,
    bias,
    cotangent,
    hidden,
    weight_grad,
    bias_grad,
    input_gradient,
    block,
    scale,
    panel,
    acc,
    share,
    grads,
    back_own,
    back_send,
    back_row,
    deep_send,
    deep_recv,
    w_send,
    w_col,
    w_mid,
    w_row,
    w_deep,
    w_out,
    block_s,
    panel_s,
    panel_r,
    share_s,
    share_r,
    grads_s,
    grads_r,
    back_s,
    back_r,
    deep_s,
    deep_r,
    wc_s,
    wc_r,
    wr_s,
    wr_r,
    wd_s,
    wd_r,
    wg_s,
    wg_r,
    wo_s,
    wo_r,
):
    rows, cols, depths = sizes
    nodes = features.shape[0]
    me_r, me_c, me_d = (lax.axis_index(name) for name in ("row", "col", "depth"))
    f32, bf16 = jnp.float32, jnp.bfloat16

    def row_of(j):
        return lax.rem(me_r + j, rows)

    def col_of(m):
        return lax.rem(me_c + m, cols)

    def deep_of(k):
        return lax.rem(me_d + k, depths)

    def send(src, dst, send_sem, recv_sem, **peer):
        return pltpu.make_async_remote_copy(
            src_ref=src,
            dst_ref=dst,
            send_sem=send_sem,
            recv_sem=recv_sem,
            device_id=peer,
            device_id_type=pl.DeviceIdType.MESH,
        )

    sent = []

    def start(*args, **peer):
        copy = send(*args, **peer)
        copy.start()
        sent.append(copy)

    deep_order = sorted(range(1, depths), key=lambda k: (min(k, depths - k), k))

    bring = pltpu.make_async_copy(block_hbm, block, block_s)
    bring.start()
    barrier = pltpu.get_barrier_semaphore()
    for m in range(1, cols):
        pl.semaphore_signal(barrier, inc=1, device_id={"col": col_of(m)}, device_id_type=pl.DeviceIdType.MESH)
    for j in range(1, rows):
        pl.semaphore_signal(barrier, inc=1, device_id={"row": row_of(j)}, device_id_type=pl.DeviceIdType.MESH)
    for k in range(1, depths):
        pl.semaphore_signal(barrier, inc=1, device_id={"depth": deep_of(k)}, device_id_type=pl.DeviceIdType.MESH)
    mine = me_r * depths + me_d
    node_scale = lax.rsqrt(degree[...].astype(f32))
    scale[...] = jnp.broadcast_to(node_scale, features.shape[::-1]).T
    scaled = (features[...].astype(f32) * scale[...]).astype(bf16)
    panel[mine] = scaled
    pl.semaphore_wait(barrier, cols + rows + depths - 3)

    for k in deep_order:
        start(panel.at[mine], panel.at[mine], panel_s.at[k, 0], panel_r.at[mine], depth=deep_of(k))
    for j in range(1, rows):
        start(panel.at[mine], panel.at[mine], panel_s.at[0, j], panel_r.at[mine], row=row_of(j))

    def product(q):
        at = pl.ds(pl.multiple_of(q * nodes, nodes), nodes)
        return jnp.dot(block[:, at], panel[q], preferred_element_type=f32)

    bring.wait()
    acc[...] = product(mine)
    for k in deep_order:
        q = me_r * depths + deep_of(k)
        send(panel.at[q], panel.at[q], panel_s.at[k, 0], panel_r.at[q], depth=deep_of(k)).wait_recv()
        for j in range(1, rows):
            start(panel.at[q], panel.at[q], panel_s.at[k, j], panel_r.at[q], row=row_of(j))
        acc[...] += product(q)
    for k in [0] + deep_order:
        for j in range(1, rows):
            q = row_of(j) * depths + deep_of(k)
            send(panel.at[q], panel.at[q], panel_s.at[k, j], panel_r.at[q], row=row_of(j)).wait_recv()
            acc[...] += product(q)

    def acc_of(c):
        return acc.at[pl.ds(pl.multiple_of(c * nodes, nodes), nodes)]

    for m in range(1, cols):
        start(acc_of(col_of(m)), share.at[m - 1], share_s.at[m - 1], share_r.at[m - 1], col=col_of(m))
    aggregate = acc_of(me_c)[...]
    for m in range(1, cols):
        send(acc_of(me_c), share.at[m - 1], share_s.at[m - 1], share_r.at[m - 1], col=col_of(m)).wait_recv()
        aggregate = aggregate + share[m - 1]

    mixed = (scale[...] * (aggregate + scaled.astype(f32))).astype(bf16)
    pre_act = jnp.dot(mixed, weight[...], preferred_element_type=f32) + bias[...]
    activated, slope_value = silu_parts(pre_act)
    hidden[...] = activated.astype(bf16)
    pre_grad = (cotangent[...].astype(f32) * slope_value).astype(bf16)
    agg_grad = lax.dot_general(
        pre_grad, weight[...], (((1,), (1,)), ((), ())), preferred_element_type=f32
    ).astype(bf16)
    scaled_grad = (agg_grad.astype(f32) * scale[...]).astype(bf16)
    grads[me_c] = scaled_grad
    for m in range(1, cols):
        start(grads.at[me_c], grads.at[me_c], grads_s.at[m - 1], grads_r.at[m - 1], col=col_of(m))

    w_part = lax.dot_general(mixed, pre_grad, (((0,), (0,)), ((), ())), preferred_element_type=f32)
    b_part = jnp.sum(pre_grad.astype(f32).reshape(nodes // 8, 8, pre_grad.shape[1]), axis=0)
    band = w_part.shape[0] // (cols * rows)
    for c in range(cols):
        for r in range(rows):
            first = (c * rows + r) * band
            w_send[c, r, :8] = b_part
            w_send[c, r, 8:] = w_part[first : first + band]
    for m in range(1, cols):
        start(w_send.at[col_of(m)], w_col.at[me_c], wc_s.at[m - 1], wc_r.at[m - 1], col=col_of(m))
    w_col[me_c] = w_send[me_c]

    for m in range(1, cols):
        c = lax.rem(me_c + cols - m, cols)
        send(grads.at[c], grads.at[c], grads_s.at[m - 1], grads_r.at[m - 1], col=col_of(m)).wait_recv()
    turned = grads[...].reshape(cols * nodes, scaled_grad.shape[1]).T

    def total(buffer, count):
        value = buffer[0]
        for i in range(1, count):
            value = value + buffer[i]
        return value

    for m in range(1, cols):
        c = lax.rem(me_c + cols - m, cols)
        send(w_send.at[c], w_col.at[c], wc_s.at[m - 1], wc_r.at[m - 1], col=col_of(m)).wait_recv()
    w_mid[...] = total(w_col, cols)
    for j in range(1, rows):
        start(w_mid.at[row_of(j)], w_row.at[me_r], wr_s.at[j - 1], wr_r.at[j - 1], row=row_of(j))
    w_row[me_r] = w_mid[me_r]

    def back_terms(k):
        for j in list(range(1, rows)) + [0]:
            q = row_of(j) * depths + deep_of(k)
            at = pl.ds(pl.multiple_of(q * nodes, nodes), nodes)
            term = jnp.dot(turned, block[:, at], preferred_element_type=f32)
            if j == 0:
                back_own[k] = term
            else:
                back_send[k, j - 1] = term.astype(bf16)
                start(
                    back_send.at[k, j - 1],
                    back_row.at[k, j - 1],
                    back_s.at[k, j - 1],
                    back_r.at[k, j - 1],
                    row=row_of(j),
                )

    back_order = deep_order + [0]
    back_terms(back_order[0])
    for j in range(1, rows):
        r = row_of(rows - j)
        send(w_mid.at[r], w_row.at[r], wr_s.at[j - 1], wr_r.at[j - 1], row=row_of(j)).wait_recv()
    w_deep[me_d] = total(w_row, rows)
    for k in range(1, depths):
        start(w_deep.at[me_d], w_deep.at[me_d], wd_s.at[k - 1], wd_r.at[k - 1], depth=deep_of(k))
    for k in back_order[1:]:
        back_terms(k)
    for k in range(1, depths):
        send(
            w_deep.at[me_d], w_deep.at[deep_of(depths - k)], wd_s.at[k - 1], wd_r.at[k - 1], depth=deep_of(k)
        ).wait_recv()
    w_total = total(w_deep, depths) * grad_norm
    w_out[me_c, me_r] = w_total[8:]
    bias_grad[...] = jnp.sum(w_total[:8], axis=0, keepdims=True)
    for j in range(1, rows):
        start(w_out.at[me_c, me_r], w_out.at[me_c, me_r], wg_s.at[j - 1], wg_r.at[j - 1], row=row_of(j))

    def row_sum(k):
        value = back_own[k]
        for j in range(1, rows):
            send(
                back_send.at[k, j - 1],
                back_row.at[k, j - 1],
                back_s.at[k, j - 1],
                back_r.at[k, j - 1],
                row=row_of(j),
            ).wait_recv()
            value = value + back_row[k, j - 1].astype(f32)
        return value

    for k in deep_order:
        deep_send[k - 1] = row_sum(k).astype(bf16)
        start(deep_send.at[k - 1], deep_recv.at[k - 1], deep_s.at[k - 1], deep_r.at[k - 1], depth=deep_of(k))

    back = row_sum(0)

    for j in range(1, rows):
        r = row_of(rows - j)
        send(w_out.at[me_c, r], w_out.at[me_c, r], wg_s.at[j - 1], wg_r.at[j - 1], row=row_of(j)).wait_recv()
    for m in range(1, cols):
        start(w_out.at[me_c], w_out.at[me_c], wo_s.at[m - 1], wo_r.at[m - 1], col=col_of(m))

    for k in range(1, depths):
        send(
            deep_send.at[k - 1], deep_recv.at[k - 1], deep_s.at[k - 1], deep_r.at[k - 1], depth=deep_of(k)
        ).wait_recv()
        back = back + deep_recv[k - 1].astype(f32)
    input_gradient[...] = (scale[...] * (back.T + grads[me_c].astype(f32))).astype(bf16)

    for m in range(1, cols):
        c = lax.rem(me_c + cols - m, cols)
        send(w_out.at[c], w_out.at[c], wo_s.at[m - 1], wo_r.at[m - 1], col=col_of(m)).wait_recv()
    for c in range(cols):
        for r in range(rows):
            first = (c * rows + r) * band
            weight_grad[first : first + band] = w_out[c, r]
    for copy in sent:
        copy.wait_send()


def finish_kernel(*refs):
    count = len(refs) // 2
    for i in range(count):
        refs[count + i][...] = refs[i][...]


def finish(*arrays):
    vmem = pl.BlockSpec(memory_space=pltpu.VMEM)
    return pl.pallas_call(
        finish_kernel,
        out_shape=tuple(jax.ShapeDtypeStruct(a.shape, a.dtype) for a in arrays),
        in_specs=[vmem] * len(arrays),
        out_specs=(vmem,) * len(arrays),
    )(*arrays)


def run_layer(sizes, grad_norm, block, features, degree, weight, bias, cotangent):
    rows, cols, depths = sizes
    nodes, width = features.shape
    wide = weight.shape[1]
    band = width // (cols * rows)
    f32, bf16 = jnp.float32, jnp.bfloat16

    def dma(*shape):
        return [pltpu.SemaphoreType.DMA(shape)] * 2

    return pl.pallas_call(
        functools.partial(layer_kernel, sizes, grad_norm),
        out_shape=(
            jax.ShapeDtypeStruct((nodes, wide), bf16),
            jax.ShapeDtypeStruct((width, wide), f32),
            jax.ShapeDtypeStruct((1, wide), f32),
            jax.ShapeDtypeStruct((nodes, width), bf16),
        ),
        in_specs=[pl.BlockSpec(memory_space=pl.ANY)] + [pl.BlockSpec(memory_space=pltpu.VMEM)] * 5,
        out_specs=(pl.BlockSpec(memory_space=pltpu.VMEM),) * 4,
        scratch_shapes=[
            pltpu.VMEM(block.shape, bf16),
            pltpu.VMEM((nodes, width), f32),
            pltpu.VMEM((rows * depths, nodes, width), bf16),
            pltpu.VMEM((cols * nodes, width), f32),
            pltpu.VMEM((cols - 1, nodes, width), f32),
            pltpu.VMEM((cols, nodes, width), bf16),
            pltpu.VMEM((depths, width, nodes), f32),
            pltpu.VMEM((depths, rows - 1, width, nodes), bf16),
            pltpu.VMEM((depths, rows - 1, width, nodes), bf16),
            pltpu.VMEM((depths - 1, width, nodes), bf16),
            pltpu.VMEM((depths - 1, width, nodes), bf16),
            pltpu.VMEM((cols, rows, band + 8, wide), f32),
            pltpu.VMEM((cols, rows, band + 8, wide), f32),
            pltpu.VMEM((rows, band + 8, wide), f32),
            pltpu.VMEM((rows, band + 8, wide), f32),
            pltpu.VMEM((depths, band + 8, wide), f32),
            pltpu.VMEM((cols, rows, band, wide), f32),
            pltpu.SemaphoreType.DMA(()),
            pltpu.SemaphoreType.DMA((depths, rows)),
            pltpu.SemaphoreType.DMA((rows * depths,)),
            *dma(cols - 1),
            *dma(cols - 1),
            *dma(depths, rows - 1),
            *dma(depths - 1),
            *dma(cols - 1),
            *dma(rows - 1),
            *dma(depths - 1),
            *dma(rows - 1),
            *dma(cols - 1),
        ],
        compiler_params=pltpu.CompilerParams(
            collective_id=0, has_side_effects=True, vmem_limit_bytes=56 * 1024 * 1024
        ),
    )(block, features, degree, weight, bias, cotangent)


def local(features, degree, tiles, tile_rows, tile_cols, tile_count, weight, bias, cotangent):
    node_dev, feature_width = features.shape
    tile_size = tiles.shape[-1]
    slot_total = tiles.shape[3]
    sizes = tuple(lax.axis_size(name) for name in ("row", "col", "depth"))
    row_tiles = sizes[1] * node_dev // tile_size
    span = sizes[0] * sizes[2] * node_dev // tile_size
    grad_norm = (node_dev * sizes[0] * sizes[1] * sizes[2]) ** (-0.5)
    block = build_block(
        tiles.reshape(slot_total, tile_size, tile_size),
        tile_rows.reshape(slot_total),
        tile_cols.reshape(slot_total),
        tile_count.reshape(1),
        row_tiles,
        span,
    )
    results = run_layer(
        sizes, grad_norm, block, features, degree.reshape(1, -1), weight, bias.reshape(1, -1), cotangent
    )
    hidden, weight_grad, bias_grad, input_gradient = finish(*results)
    return (hidden, weight_grad, bias_grad.reshape(-1), input_gradient)


def solution(mesh):
    return jax.shard_map(
        local,
        mesh=mesh,
        in_specs=(
            P(("row", "col", "depth"), None),
            P(("row", "col", "depth")),
            P("row", "col", "depth", None, None, None),
            P("row", "col", "depth", None),
            P("row", "col", "depth", None),
            P("row", "col", "depth"),
            P(),
            P(),
            P(("row", "col", "depth"), None),
        ),
        out_specs=(P(("row", "col", "depth"), None), P(), P(), P(("row", "col", "depth"), None)),
        check_vma=False,
    )
```
